32 devices in a mesh: grp: 2 (over y), tm: 4 (over z), row: 2 (over x), col: 2 (over core).
Axes of the slice: x: 2, y: 2, z: 4, core: 2. Of those that a mesh axis runs over, the one named last changes fastest.
Arguments:
- frames: bfloat16 [8, 16, 9216], P(('grp', 'tm'), 'row', 'col'), parts along dimension 0, may hold values from -6 to 6
- owner_map: int32 [8], P('grp'), parts along dimension 0, may hold values from 0 to 3, each once
- valid_blocks: int32 [8, 2, 36], P(('grp', 'tm'), 'row', 'col'), parts along dimension 0, may hold values 0 or 1
- deblock_weight: bfloat16 [288, 32], replicated, may hold values from -0.375 to 0.375
- deblock_bias: float32 [32], replicated, may hold values from -3 to 3
- encoder_weight: bfloat16 [864, 64], replicated, may hold values from -0.21875 to 0.21875
- encoder_bias: float32 [64], replicated, may hold values from -3 to 3
Outputs:
- encoded: bfloat16 [6, 2, 4, 9216], P('grp', 'row', 'tm', 'col'), parts along dimension 0
The draws below stay inside these ranges and needn't reach their ends.
There are 2 independent parts, one for each index of `grp`. The reference program is written for one: setup_inputs(seed, part) draws one part's arguments, and reference() takes and returns one part's arrays. A program takes and returns all parts, laid end to end along the dimension named above; an argument that names none is the same for every part. Nothing has to cross between parts.
Inputs may be any that keep to these rules, and one draw needn't show every extreme that they name: `owner_map`: each time index is held by exactly one slot.
All inputs are finite; a program needn't handle non-finite values. No bound on the sum of `valid_blocks` on one device may be relied on, other than what follows from the above.
Results may differ from the reference program's by a relative error of at most 0.0085.
Values may be sent and summed in bfloat16 or wider, within the bound.
A program may use at most 64 MiB of HBM per device.

```python
import jax
import jax.numpy as jnp
from jax import lax

CH = 32
OUTC = 64
BAND = 1
ROWS = 16
COLS = 288
FRAMES = 4
OUT_FRAMES = 3
N_TM = 4
N_ROW = 2


def with_ends(array, stream_key, low, top_value):
    dims = array.shape
    spot = [jax.random.randint(jax.random.fold_in(stream_key, axis), (), 0, dims[axis]) for axis in range(len(dims))]
    array = array.at[tuple(spot)].set(low)
    longest = dims.index(max(dims))
    spot[longest] = (spot[longest] + 1) % dims[longest]
    return array.at[tuple(spot)].set(top_value)


def steps_of(key, shape, split, least, top_value):
    def one(position, shards_of):
        draws = jax.random.uniform(jax.random.fold_in(jax.random.fold_in(key, 6), position), (shards_of,), jnp.float32, least / len(split), top_value / len(split))
        return jnp.repeat(jnp.exp(draws), shape[position] // shards_of).reshape((-1,) + (1,) * (len(shape) - position - 1))

    level = one(*split[0])
    for cut in split[1:]:
        level = level * one(*cut)
    return level


def normal_values(own_key, shape, deviation, reach, split=(), held_as=jnp.bfloat16):
    level = steps_of(own_key, shape, split, -0.22, 0.18) if split else 1.0
    values = jax.random.normal(own_key, shape, jnp.float32) * deviation * level
    return jnp.minimum(jnp.maximum(values, -reach), reach).astype(held_as)


def setup_inputs(seed: int = 0, part: int = 0) -> dict:
    seeds = jax.random.split(jax.random.key(seed), 8)
    own_keys = jax.random.split(jax.random.fold_in(seeds[7], part), 8)
    return {
        "frames": normal_values(own_keys[0], (FRAMES, ROWS, COLS * CH), 1.0, 6.0, ((0, 4), (1, 2), (2, 2))),
        "owner_map": jax.random.permutation(own_keys[1], FRAMES).astype(jnp.int32),
        "valid_blocks": with_ends((jax.random.randint(own_keys[2], (FRAMES, ROWS // 8, COLS // 8), 0, 4) < 3).astype(jnp.int32), jax.random.fold_in(own_keys[2], 1), 0, 1),
        "deblock_weight": normal_values(seeds[3], (9 * CH, CH), (9 * CH) ** -0.5, 0.375),
        "deblock_bias": normal_values(seeds[4], (CH,), 0.5, 3.0, (), jnp.float32),
        "encoder_weight": normal_values(seeds[5], (27 * CH, OUTC), (27 * CH) ** -0.5, 0.21875),
        "encoder_bias": normal_values(seeds[6], (OUTC,), 0.5, 3.0, (), jnp.float32),
    }


def conv_taps(padded, weight, height, extent):
    channels = padded.shape[-1]
    summed = jnp.zeros((), jnp.float32)
    for row_step in range(3):
        stripe = padded[..., row_step:row_step + height, :, :]
        patches = jnp.concatenate([stripe[..., col_step:col_step + extent, :] for col_step in range(3)], axis=-1)
        patches = patches.reshape(-1, 3 * channels)
        kernel = weight[row_step * 3 * channels:(row_step + 1) * 3 * channels]
        summed = summed + jnp.dot(patches, kernel, preferred_element_type=jnp.float32)
    return summed


def pool_pairs(source):
    leading = source.shape[:-3]
    height, extent, channels = source.shape[-3:]
    grouped = source.astype(jnp.float32).reshape(leading + (height // 2, 2, extent // 2, 2, channels))
    depth = len(leading)
    return jnp.mean(grouped, axis=(depth + 1, depth + 3)).astype(jnp.bfloat16)


def reference(frames, owner_map, valid_blocks, deblock_weight, deblock_bias, encoder_weight, encoder_bias):
    def clean_one(item):
        frame, blocks = item
        image = frame.reshape(ROWS, COLS, CH)
        framed = jnp.pad(image, ((1, 1), (1, 1), (0, 0)))
        filtered = conv_taps(framed, deblock_weight, ROWS, COLS).reshape(ROWS, COLS, CH) + deblock_bias
        coverage = jnp.broadcast_to(blocks.astype(jnp.float32)[:, None, :, None], (ROWS // 8, 8, COLS // 8, 8)).reshape(ROWS, COLS, 1)
        cleaned = (image.astype(jnp.float32) + coverage * filtered).astype(jnp.bfloat16)
        return pool_pairs(cleaned)

    pooled = lax.map(clean_one, (frames, valid_blocks))
    indices = jnp.arange(FRAMES, dtype=jnp.int32)
    matches = (owner_map[None, :] == indices[:, None]).astype(jnp.int32)
    slot_of_time = jnp.sum(matches * indices[None, :], axis=1).astype(jnp.int32)
    ordered = jnp.take(pooled, slot_of_time, axis=0)

    def encode_one(output_index):
        moment = output_index + 1
        summed = jnp.zeros(((ROWS // 2) * (COLS // 2), OUTC), jnp.float32)
        for frame_lag in range(3):
            chosen = jnp.maximum(moment - frame_lag, 0).astype(jnp.int32)
            picture = lax.dynamic_index_in_dim(ordered, chosen, 0, keepdims=False)
            framed = jnp.pad(picture, ((1, 1), (1, 1), (0, 0)))
            kernel = encoder_weight[frame_lag * 9 * CH:(frame_lag + 1) * 9 * CH]
            summed = summed + conv_taps(framed, kernel, ROWS // 2, COLS // 2)
        return (summed + encoder_bias).astype(jnp.bfloat16)

    encoded = lax.map(encode_one, jnp.arange(OUT_FRAMES, dtype=jnp.int32))
    return encoded.reshape(OUT_FRAMES, N_ROW, N_TM * BAND, (COLS // 2) * OUTC)
```

```python
import functools

import jax
import jax.numpy as jnp
from jax import lax
from jax.experimental import pallas as pl
from jax.experimental.pallas import tpu as pltpu
from jax.sharding import PartitionSpec as P

CH = 32
OUTC = 64
MESH = pl.DeviceIdType.MESH
F32 = jnp.float32
BF16 = jnp.bfloat16


def place(dr, dc):
    return (dr + 1) * 3 + dc + 1


DIRECTIONS = [(dr, dc) for dr in (-1, 0, 1) for dc in (-1, 0, 1) if (dr, dc) != (0, 0)]


def iota(shape, dim):
    return lax.broadcasted_iota(jnp.int32, shape, dim)


def spread_taps(taps, spread):
    return lax.dot_general(taps, spread, (((0,), (0,)), ((), ())), preferred_element_type=F32)


def deblock_matrix(dw_ref, t_ref):
    spread = (iota((CH, 4 * CH), 1) % CH == iota((CH, 4 * CH), 0)).astype(BF16)
    tiled = spread_taps(dw_ref[...], spread)
    taps = [[tiled[(3 * a + b) * CH : (3 * a + b + 1) * CH] for b in range(3)] for a in range(3)]
    wide = [
        [sum(row[b] for b in (d - 1, d) if 0 <= b < 3) for d in range(4)]
        for row in taps
    ]
    four = [
        [0.25 * sum(wide[a][d] for a in (e - 1, e) if 0 <= a < 3) for d in range(4)]
        for e in range(4)
    ]
    block = iota((CH, 4 * CH), 1) // CH
    zero = jnp.zeros((CH, 4 * CH), F32)
    rows, cols = iota((8 * CH, 4 * CH), 0), iota((8 * CH, 4 * CH), 1)
    mean = jnp.where((rows // (2 * CH) == cols // CH) & (rows % CH == cols % CH), 0.25, 0.0).astype(BF16)
    nothing = jnp.zeros((8 * CH, 4 * CH), BF16)
    for e in range(4):
        base = e * 12 * CH

        def put(at, pixel):
            total = zero
            for o in range(4):
                d = pixel - 2 * o + 1
                if 0 <= d < 4:
                    total = jnp.where(block == o, four[e][d], total)
            t_ref[base + at * CH : base + (at + 1) * CH, : 4 * CH] = total.astype(BF16)

        for pixel in range(8):
            put(pixel, pixel)
        put(8, 8)
        put(11, -1)
        t_ref[base + 9 * CH : base + 11 * CH, : 4 * CH] = nothing[: 2 * CH]
        t_ref[base : base + 8 * CH, 4 * CH :] = mean if e in (1, 2) else nothing
        t_ref[base + 8 * CH : base + 12 * CH, 4 * CH :] = nothing[: 4 * CH]


def encoder_matrix(ew_ref, t_ref):
    width = 4 * OUTC
    spread = (iota((OUTC, width), 1) % OUTC == iota((OUTC, width), 0)).astype(BF16)
    block = iota((CH, width), 1) // OUTC
    zero = jnp.zeros((CH, width), F32)
    nothing = jnp.zeros((2 * CH, width), BF16)
    everything = spread_taps(ew_ref[...], spread)
    for lag in range(3):
        tiled = everything[lag * 9 * CH : (lag + 1) * 9 * CH]
        for dy in range(3):
            base = dy * 8 * CH
            left = lag * width

            def put(at, pixel):
                total = zero
                for o in range(4):
                    d = pixel - o + 1
                    if 0 <= d < 3:
                        tap = tiled[(3 * dy + d) * CH : (3 * dy + d + 1) * CH]
                        total = jnp.where(block == o, tap, total)
                t_ref[base + at * CH : base + (at + 1) * CH, left : left + width] = total.astype(BF16)

            for pixel in range(4):
                put(pixel, pixel)
            put(4, 4)
            put(7, -1)
            t_ref[base + 5 * CH : base + 7 * CH, left : left + width] = nothing


def kernel(
    sizes,
    owner_ref,
    raw_ref,
    x_ref,
    vb_ref,
    dw_ref,
    db_ref,
    ew_ref,
    eb_ref,
    out_ref,
    ext,
    halo,
    edge,
    flags,
    tdeb,
    tenc,
    pooled,
    bands_in,
    product,
    send_sem,
    recv_sem,
    band_send,
    band_recv,
):
    n, nr, nc = sizes
    height, groups, _ = x_ref.shape
    padded = ext.shape[1]
    half = height // 2
    stride = half // n
    me = lax.axis_index("tm")
    r = lax.axis_index("row")
    c = lax.axis_index("col")

    halo[...] = jnp.zeros_like(halo)
    edge[...] = jnp.zeros_like(edge)
    flags[...] = jnp.zeros_like(flags)

    def exists(dr, dc):
        found = None
        for step, at, count in ((dr, r, nr), (dc, c, nc)):
            if step:
                inside = at > 0 if step < 0 else at < count - 1
                found = inside if found is None else jnp.logical_and(found, inside)
        return found

    def copies(dr, dc):
        here, there = place(dr, dc), place(-dr, -dc)
        to = {}
        if dr:
            to["row"] = r + dr
        if dc:
            to["col"] = c + dc
        if dc:
            lanes = pl.ds(0, 4 * CH) if dc < 0 else pl.ds(raw_ref.shape[1] - 4 * CH, 4 * CH)
            src, dst = raw_ref.at[:, lanes], edge.at[there]
        else:
            src = x_ref.at[pl.ds(0 if dr < 0 else height - 3, 3)]
            dst = halo.at[1 if dr < 0 else 0]
        return [
            pltpu.make_async_remote_copy(
                src_ref=a, dst_ref=b, send_sem=send_sem.at[here, k], recv_sem=recv_sem.at[there, k],
                device_id=to, device_id_type=MESH,
            )
            for k, (a, b) in enumerate(((src, dst), (vb_ref, flags.at[there])))
        ]

    barrier = pltpu.get_barrier_semaphore()
    for dr, dc in DIRECTIONS:
        to = {}
        if dr:
            to["row"] = r + dr
        if dc:
            to["col"] = c + dc

        @pl.when(exists(dr, dc))
        def _():
            pl.semaphore_signal(barrier, inc=1, device_id=to, device_id_type=MESH)

    for d in range(1, n):
        pl.semaphore_signal(
            barrier, inc=1, device_id={"tm": lax.rem(me + d, n)}, device_id_type=MESH
        )
    tall = (r > 0).astype(jnp.int32) + (r < nr - 1).astype(jnp.int32) + 1
    broad = (c > 0).astype(jnp.int32) + (c < nc - 1).astype(jnp.int32) + 1
    pl.semaphore_wait(barrier, tall * broad - 1 + n - 1)

    for dr, dc in DIRECTIONS:

        @pl.when(exists(dr, dc))
        def _():
            for copy in copies(dr, dc):
                copy.start()

    deblock_matrix(dw_ref, tdeb)
    ext[...] = jnp.zeros_like(ext)
    ext[3 : 3 + height, :groups, : 8 * CH] = x_ref[...].astype(F32)

    for dr, dc in DIRECTIONS:

        @pl.when(exists(dr, dc))
        def _():
            for copy in copies(-dr, -dc):
                copy.wait_recv()

    ext[:3, :groups, : 8 * CH] = halo[0].astype(F32)
    ext[3 + height :, :groups, : 8 * CH] = halo[1].astype(F32)
    for dc, at, lanes in ((-1, padded - 1, 4 * CH), (1, groups, 0)):
        middle = edge[place(0, dc)].astype(F32)
        top = edge[place(-1, dc)].astype(F32)
        low = edge[place(1, dc)].astype(F32)
        lines = [top[height - 3 + k : height - 2 + k] for k in range(3)]
        lines += [middle[k : k + 1] for k in range(height)]
        lines += [low[k : k + 1] for k in range(3)]
        for k, line in enumerate(lines):
            ext[k, at : at + 1, lanes : lanes + 4 * CH] = line

    lane = iota((padded, 4 * CH), 1)
    for k in range(height + 6):
        before = pltpu.roll(ext[k, :, 4 * CH : 8 * CH], 1, 0)
        after = pltpu.roll(ext[k, :, : 4 * CH], padded - 1, 0)
        ext[k, :, 8 * CH :] = jnp.where(
            lane >= 3 * CH, before, jnp.where(lane < CH, after, 0.0)
        )

    lhs = jnp.concatenate(
        [
            jnp.concatenate([ext[2 * k + e] for e in range(4)], axis=1)
            for k in range(half + 2)
        ],
        axis=0,
    ).astype(BF16)
    conv = jnp.dot(lhs, tdeb[...], preferred_element_type=F32)

    def column(line, left, right):
        spot = iota((padded, groups), 0)
        own = jnp.sum(
            jnp.where(spot == iota((padded, groups), 1), jnp.broadcast_to(line, (padded, groups)), 0.0),
            axis=1, keepdims=True,
        )
        spot = iota((padded, 1), 0)
        own = jnp.where(spot == padded - 1, jnp.broadcast_to(left[:, groups - 1 :], (padded, 1)), own)
        return jnp.where(spot == groups, jnp.broadcast_to(right[:, :1], (padded, 1)), own)

    blocks = vb_ref.shape[0]

    def flag_row(dr, k):
        rows = [
            vb_ref[k : k + 1, :] if (dr, dc) == (0, 0) else flags[place(dr, dc), k : k + 1, :]
            for dc in (-1, 0, 1)
        ]
        left, line, right = [row.astype(F32) for row in rows]
        return column(line, left, right)

    masks = [flag_row(-1, blocks - 1)] + [flag_row(0, k) for k in range(blocks)] + [flag_row(1, 0)]
    deblock_bias = jnp.concatenate([db_ref[...]] * 4, axis=1)
    per = half // blocks
    for k in range(half + 2):
        part = conv[k * padded : (k + 1) * padded]
        which = 0 if k == 0 else blocks + 1 if k == half + 1 else 1 + (k - 1) // per
        pooled[k] = (
            part[:, 4 * CH :] + masks[which] * (part[:, : 4 * CH] + deblock_bias)
        ).astype(BF16)

    def band_copy(d):
        to = lax.rem(me + d, n)
        return pltpu.make_async_remote_copy(
            src_ref=pooled.at[pl.ds(to * stride, stride + 2)],
            dst_ref=bands_in.at[me],
            send_sem=band_send.at[d],
            recv_sem=band_recv.at[d],
            device_id={"tm": to},
            device_id_type=MESH,
        )

    def band_arrival(d):
        source = lax.rem(me + n - d, n)
        return pltpu.make_async_remote_copy(
            src_ref=pooled.at[pl.ds(0, stride + 2)],
            dst_ref=bands_in.at[source],
            send_sem=band_send.at[d],
            recv_sem=band_recv.at[d],
            device_id={"tm": source},
            device_id_type=MESH,
        )

    for d in range(1, n):
        band_copy(d).start()
    bands_in[me] = pooled[pl.ds(me * stride, stride + 2)]
    encoder_matrix(ew_ref, tenc)
    for d in range(1, n):
        band_arrival(d).wait_recv()

    rows = []
    for s in range(n):
        lines = []
        for k in range(stride + 2):
            own = bands_in[s, k].astype(F32)
            side = jnp.where(
                lane >= 3 * CH,
                pltpu.roll(own, 1, 0),
                jnp.where(lane < CH, pltpu.roll(own, padded - 1, 0), 0.0),
            )
            lines.append(jnp.concatenate([own, side], axis=1))
        for k in range(stride):
            rows.append(jnp.concatenate(lines[k : k + 3], axis=1))
    lhs = jnp.concatenate(rows, axis=0).astype(BF16)
    found = jnp.dot(lhs, tenc[...], preferred_element_type=F32)
    product[...] = found.reshape(product.shape)

    slots = []
    for t in range(n):
        if n <= 8:
            slot = jnp.int32(0)
            for s in range(n):
                slot = jnp.where(owner_ref[s] == t, s, slot)
        else:
            slot = lax.fori_loop(
                0, n, lambda s, held: jnp.where(owner_ref[s] == t, s, held), jnp.int32(0)
            )
        slots.append(slot)
    width = 4 * OUTC
    encoder_bias = jnp.concatenate([eb_ref[...]] * 4, axis=1)
    for t in range(1, n):
        for k in range(stride):
            total = encoder_bias
            for lag in range(3):
                total = total + product[slots[max(t - lag, 0)], k, :, lag * width : (lag + 1) * width]
            out_ref[t - 1, k] = total[:groups].astype(BF16)

    for dr, dc in DIRECTIONS:

        @pl.when(exists(dr, dc))
        def _():
            for copy in copies(dr, dc):
                copy.wait_send()

    for d in range(1, n):
        band_copy(d).wait_send()


def on_device(
    sizes, frames, owner_map, valid_blocks, deblock_weight, deblock_bias, encoder_weight, encoder_bias
):
    n = sizes[0]
    _, height, lanes = frames.shape
    raw = frames[0]
    groups = lanes // (8 * CH)
    padded = -(-(groups + 2) // 8) * 8
    blocks = valid_blocks.shape[1]
    half = height // 2
    stride = half // n
    x = raw.reshape(height, groups, 8 * CH)
    vmem = pl.BlockSpec(memory_space=pltpu.VMEM)
    encoded = pl.pallas_call(
        functools.partial(kernel, sizes),
        out_shape=jax.ShapeDtypeStruct((n - 1, stride, groups, 4 * OUTC), BF16),
        in_specs=[pl.BlockSpec(memory_space=pltpu.SMEM), pl.BlockSpec(memory_space=pl.ANY)] + [vmem] * 6,
        out_specs=vmem,
        scratch_shapes=[
            pltpu.VMEM((height + 6, padded, 12 * CH), F32),
            pltpu.VMEM((2, 3, groups, 8 * CH), BF16),
            pltpu.VMEM((9, height, 4 * CH), BF16),
            pltpu.VMEM((9, blocks, groups), jnp.int32),
            pltpu.VMEM((48 * CH, 8 * CH), BF16),
            pltpu.VMEM((24 * CH, 12 * OUTC), BF16),
            pltpu.VMEM((half + 2, padded, 4 * CH), BF16),
            pltpu.VMEM((n, stride + 2, padded, 4 * CH), BF16),
            pltpu.VMEM((n, stride, padded, 12 * OUTC), F32),
            pltpu.SemaphoreType.DMA((9, 2)),
            pltpu.SemaphoreType.DMA((9, 2)),
            pltpu.SemaphoreType.DMA((n,)),
            pltpu.SemaphoreType.DMA((n,)),
        ],
        compiler_params=pltpu.CompilerParams(
            collective_id=0, has_side_effects=True, vmem_limit_bytes=40 * 1024 * 1024
        ),
    )(
        owner_map, raw, x, valid_blocks[0], deblock_weight.T, deblock_bias[None], encoder_weight.T,
        encoder_bias[None],
    )
    return encoded.reshape(n - 1, 1, stride, groups * 4 * OUTC)


def solution(mesh):
    sizes = (mesh.shape["tm"], mesh.shape["row"], mesh.shape["col"])
    return jax.shard_map(
        functools.partial(on_device, sizes),
        mesh=mesh,
        in_specs=(
            P(("grp", "tm"), "row", "col"),
            P("grp"),
            P(("grp", "tm"), "row", "col"),
            P(),
            P(),
            P(),
            P(),
        ),
        out_specs=P("grp", "row", "tm", "col"),
        check_vma=False,
    )
```

```python
import functools

import jax
import jax.numpy as jnp
from jax import lax
from jax.experimental import pallas as pl
from jax.experimental.pallas import tpu as pltpu
from jax.sharding import PartitionSpec as P

CH = 32
OUTC = 64
MESH = pl.DeviceIdType.MESH
F32 = jnp.float32
BF16 = jnp.bfloat16


def place(dr, dc):
    return (dr + 1) * 3 + dc + 1


DIRECTIONS = [(dr, dc) for dr in (-1, 0, 1) for dc in (-1, 0, 1) if (dr, dc) != (0, 0)]


def iota(shape, dim):
    return lax.broadcasted_iota(jnp.int32, shape, dim)


def spread_taps(taps, spread):
    return lax.dot_general(taps, spread, (((0,), (0,)), ((), ())), preferred_element_type=F32)


def deblock_matrix(dw_ref, t_ref):
    spread = (iota((CH, 4 * CH), 1) % CH == iota((CH, 4 * CH), 0)).astype(BF16)
    tiled = spread_taps(dw_ref[...], spread)
    taps = [[tiled[(3 * a + b) * CH : (3 * a + b + 1) * CH] for b in range(3)] for a in range(3)]
    wide = [
        [sum(row[b] for b in (d - 1, d) if 0 <= b < 3) for d in range(4)]
        for row in taps
    ]
    four = [
        [0.25 * sum(wide[a][d] for a in (e - 1, e) if 0 <= a < 3) for d in range(4)]
        for e in range(4)
    ]
    block = iota((CH, 4 * CH), 1) // CH
    zero = jnp.zeros((CH, 4 * CH), F32)
    rows, cols = iota((8 * CH, 4 * CH), 0), iota((8 * CH, 4 * CH), 1)
    mean = jnp.where((rows // (2 * CH) == cols // CH) & (rows % CH == cols % CH), 0.25, 0.0).astype(BF16)
    nothing = jnp.zeros((8 * CH, 4 * CH), BF16)
    for e in range(4):
        base = e * 12 * CH

        def put(at, pixel):
            total = zero
            for o in range(4):
                d = pixel - 2 * o + 1
                if 0 <= d < 4:
                    total = jnp.where(block == o, four[e][d], total)
            t_ref[base + at * CH : base + (at + 1) * CH, : 4 * CH] = total.astype(BF16)

        for pixel in range(8):
            put(pixel, pixel)
        put(8, 8)
        put(11, -1)
        t_ref[base + 9 * CH : base + 11 * CH, : 4 * CH] = nothing[: 2 * CH]
        t_ref[base : base + 8 * CH, 4 * CH :] = mean if e in (1, 2) else nothing
        t_ref[base + 8 * CH : base + 12 * CH, 4 * CH :] = nothing[: 4 * CH]


def encoder_matrix(ew_ref, t_ref):
    width = 4 * OUTC
    spread = (iota((OUTC, width), 1) % OUTC == iota((OUTC, width), 0)).astype(BF16)
    block = iota((CH, width), 1) // OUTC
    zero = jnp.zeros((CH, width), F32)
    nothing = jnp.zeros((2 * CH, width), BF16)
    everything = spread_taps(ew_ref[...], spread)
    for lag in range(3):
        tiled = everything[lag * 9 * CH : (lag + 1) * 9 * CH]
        for dy in range(3):
            base = dy * 8 * CH
            left = lag * width

            def put(at, pixel):
                total = zero
                for o in range(4):
                    d = pixel - o + 1
                    if 0 <= d < 3:
                        tap = tiled[(3 * dy + d) * CH : (3 * dy + d + 1) * CH]
                        total = jnp.where(block == o, tap, total)
                t_ref[base + at * CH : base + (at + 1) * CH, left : left + width] = total.astype(BF16)

            for pixel in range(4):
                put(pixel, pixel)
            put(4, 4)
            put(7, -1)
            t_ref[base + 5 * CH : base + 7 * CH, left : left + width] = nothing


def kernel(
    sizes,
    owner_hbm,
    raw_hbm,
    vb_hbm,
    dw_hbm,
    db_hbm,
    ew_hbm,
    eb_hbm,
    out_ref,
    owner_ref,
    raw_ref,
    vb_ref,
    dw_ref,
    db_ref,
    ew_ref,
    eb_ref,
    ext,
    outgoing,
    halo,
    edge,
    flags,
    tdeb,
    tenc,
    pooled,
    bands_in,
    product,
    load_sem,
    send_sem,
    recv_sem,
    band_send,
    band_recv,
):
    n, nr, nc = sizes
    height, width = raw_ref.shape
    groups = width // (8 * CH)
    padded = halo.shape[2]
    half = height // 2
    stride = half // n
    me = lax.axis_index("tm")
    r = lax.axis_index("row")
    c = lax.axis_index("col")

    loads = [
        pltpu.make_async_copy(a, b, load_sem.at[k])
        for k, (a, b) in enumerate(
            (
                (raw_hbm, raw_ref),
                (vb_hbm, vb_ref),
                (dw_hbm, dw_ref),
                (db_hbm, db_ref),
                (ew_hbm, ew_ref),
                (eb_hbm, eb_ref),
                (owner_hbm, owner_ref),
            )
        )
    ]
    for load in loads:
        load.start()

    halo[...] = jnp.zeros_like(halo)
    edge[...] = jnp.zeros_like(edge)
    flags[...] = jnp.zeros_like(flags)

    def exists(dr, dc):
        found = None
        for step, at, count in ((dr, r, nr), (dc, c, nc)):
            if step:
                inside = at > 0 if step < 0 else at < count - 1
                found = inside if found is None else jnp.logical_and(found, inside)
        return found

    def copies(dr, dc):
        here, there = place(dr, dc), place(-dr, -dc)
        to = {}
        if dr:
            to["row"] = r + dr
        if dc:
            to["col"] = c + dc
        if dc:
            lanes = pl.ds(0, 4 * CH) if dc < 0 else pl.ds(raw_ref.shape[1] - 4 * CH, 4 * CH)
            src, dst = raw_ref.at[:, lanes], edge.at[there]
        else:
            src = outgoing.at[0 if dr < 0 else 1]
            dst = halo.at[1 if dr < 0 else 0]
        return [
            pltpu.make_async_remote_copy(
                src_ref=a, dst_ref=b, send_sem=send_sem.at[here, k], recv_sem=recv_sem.at[there, k],
                device_id=to, device_id_type=MESH,
            )
            for k, (a, b) in enumerate(((src, dst), (vb_ref, flags.at[there])))
        ]

    barrier = pltpu.get_barrier_semaphore()
    for dr, dc in DIRECTIONS:
        to = {}
        if dr:
            to["row"] = r + dr
        if dc:
            to["col"] = c + dc

        @pl.when(exists(dr, dc))
        def _():
            pl.semaphore_signal(barrier, inc=1, device_id=to, device_id_type=MESH)

    for d in range(1, n):
        pl.semaphore_signal(
            barrier, inc=1, device_id={"tm": lax.rem(me + d, n)}, device_id_type=MESH
        )
    ext[...] = jnp.zeros_like(ext)

    def line_of(k):
        return pl.ds(k * padded, padded)

    loads[0].wait()
    for h in range(0, height, 8):
        for q in range(2 * groups):
            ext[q % 2, pl.ds((3 + h) * padded + q // 2, 8, stride=padded), :] = raw_ref[
                h : h + 8, q * 4 * CH : (q + 1) * 4 * CH
            ].astype(F32)
    for side, dr in enumerate((-1, 1)):

        @pl.when(exists(dr, 0))
        def _():
            for k in range(3):
                line = line_of(3 + k if dr < 0 else height + k)
                for j in range(2):
                    outgoing[side, k, :, j * 4 * CH : (j + 1) * 4 * CH] = ext[j, line, :].astype(BF16)

    loads[1].wait()
    tall = (r > 0).astype(jnp.int32) + (r < nr - 1).astype(jnp.int32) + 1
    broad = (c > 0).astype(jnp.int32) + (c < nc - 1).astype(jnp.int32) + 1
    pl.semaphore_wait(barrier, tall * broad - 1 + n - 1)

    for dr, dc in DIRECTIONS:

        @pl.when(exists(dr, dc))
        def _():
            for copy in copies(dr, dc):
                copy.start()

    loads[2].wait()
    loads[3].wait()
    deblock_matrix(dw_ref, tdeb)

    for dr, dc in DIRECTIONS:

        @pl.when(exists(dr, dc))
        def _():
            for copy in copies(-dr, -dc):
                copy.wait_recv()

    for side, first in ((0, 0), (1, 3 + height)):
        for k in range(3):
            for j in range(2):
                ext[j, line_of(first + k), :] = halo[
                    side, k, :, j * 4 * CH : (j + 1) * 4 * CH
                ].astype(F32)
    for dc, at, j in ((-1, padded - 1, 1), (1, groups, 0)):
        for h in range(0, height, 8):
            ext[j, pl.ds((3 + h) * padded + at, 8, stride=padded), :] = edge[
                place(0, dc), h : h + 8
            ].astype(F32)
        top = edge[place(-1, dc)].astype(F32)
        low = edge[place(1, dc)].astype(F32)
        for k in range(3):
            for line, first in ((top[height - 3 + k : height - 2 + k], k), (low[k : k + 1], 3 + height + k)):
                ext[j, first * padded + at : first * padded + at + 1, :] = line

    lane = iota((padded, 4 * CH), 1)
    for k in range(height + 6):
        before = pltpu.roll(ext[1, line_of(k), :], 1, 0)
        after = pltpu.roll(ext[0, line_of(k), :], padded - 1, 0)
        ext[2, line_of(k), :] = jnp.where(
            lane >= 3 * CH, before, jnp.where(lane < CH, after, 0.0)
        )

    lhs = jnp.concatenate(
        [
            jnp.concatenate([ext[j, line_of(2 * k + e), :] for e in range(4) for j in range(3)], axis=1)
            for k in range(half + 2)
        ],
        axis=0,
    ).astype(BF16)
    conv = jnp.dot(lhs, tdeb[...], preferred_element_type=F32)

    def column(line, left, right):
        spot = iota((padded, groups), 0)
        own = jnp.sum(
            jnp.where(spot == iota((padded, groups), 1), jnp.broadcast_to(line, (padded, groups)), 0.0),
            axis=1, keepdims=True,
        )
        spot = iota((padded, 1), 0)
        own = jnp.where(spot == padded - 1, jnp.broadcast_to(left[:, groups - 1 :], (padded, 1)), own)
        return jnp.where(spot == groups, jnp.broadcast_to(right[:, :1], (padded, 1)), own)

    blocks = vb_ref.shape[0]

    def flag_row(dr, k):
        rows = [
            vb_ref[k : k + 1, :] if (dr, dc) == (0, 0) else flags[place(dr, dc), k : k + 1, :]
            for dc in (-1, 0, 1)
        ]
        left, line, right = [row.astype(F32) for row in rows]
        return column(line, left, right)

    masks = [flag_row(-1, blocks - 1)] + [flag_row(0, k) for k in range(blocks)] + [flag_row(1, 0)]
    deblock_bias = jnp.concatenate([db_ref[...]] * 4, axis=1)
    per = half // blocks
    for k in range(half + 2):
        part = conv[k * padded : (k + 1) * padded]
        which = 0 if k == 0 else blocks + 1 if k == half + 1 else 1 + (k - 1) // per
        pooled[k] = (
            part[:, 4 * CH :] + masks[which] * (part[:, : 4 * CH] + deblock_bias)
        ).astype(BF16)

    def band_copy(d):
        to = lax.rem(me + d, n)
        return pltpu.make_async_remote_copy(
            src_ref=pooled.at[pl.ds(to * stride, stride + 2)],
            dst_ref=bands_in.at[me],
            send_sem=band_send.at[d],
            recv_sem=band_recv.at[d],
            device_id={"tm": to},
            device_id_type=MESH,
        )

    def band_arrival(d):
        source = lax.rem(me + n - d, n)
        return pltpu.make_async_remote_copy(
            src_ref=pooled.at[pl.ds(0, stride + 2)],
            dst_ref=bands_in.at[source],
            send_sem=band_send.at[d],
            recv_sem=band_recv.at[d],
            device_id={"tm": source},
            device_id_type=MESH,
        )

    for d in range(1, n):
        band_copy(d).start()
    bands_in[me] = pooled[pl.ds(me * stride, stride + 2)]
    loads[4].wait()
    encoder_matrix(ew_ref, tenc)
    loads[5].wait()
    loads[6].wait()
    for d in range(1, n):
        band_arrival(d).wait_recv()

    rows = []
    for s in range(n):
        lines = []
        for k in range(stride + 2):
            own = bands_in[s, k].astype(F32)
            side = jnp.where(
                lane >= 3 * CH,
                pltpu.roll(own, 1, 0),
                jnp.where(lane < CH, pltpu.roll(own, padded - 1, 0), 0.0),
            )
            lines.append(jnp.concatenate([own, side], axis=1))
        for k in range(stride):
            rows.append(jnp.concatenate(lines[k : k + 3], axis=1))
    lhs = jnp.concatenate(rows, axis=0).astype(BF16)
    found = jnp.dot(lhs, tenc[...], preferred_element_type=F32)
    product[...] = found.reshape(product.shape)

    slots = []
    for t in range(n):
        if n <= 8:
            slot = jnp.int32(0)
            for s in range(n):
                slot = jnp.where(owner_ref[s] == t, s, slot)
        else:
            slot = lax.fori_loop(
                0, n, lambda s, held: jnp.where(owner_ref[s] == t, s, held), jnp.int32(0)
            )
        slots.append(slot)
    width = 4 * OUTC
    encoder_bias = jnp.concatenate([eb_ref[...]] * 4, axis=1)
    for t in range(1, n):
        for k in range(stride):
            total = encoder_bias
            for lag in range(3):
                total = total + product[slots[max(t - lag, 0)], k, :, lag * width : (lag + 1) * width]
            out_ref[t - 1, k] = total[:groups].astype(BF16)

    for dr, dc in DIRECTIONS:

        @pl.when(exists(dr, dc))
        def _():
            for copy in copies(dr, dc):
                copy.wait_send()

    for d in range(1, n):
        band_copy(d).wait_send()


def on_device(
    sizes, frames, owner_map, valid_blocks, deblock_weight, deblock_bias, encoder_weight, encoder_bias
):
    n = sizes[0]
    _, height, lanes = frames.shape
    raw = frames[0]
    groups = lanes // (8 * CH)
    padded = -(-(groups + 2) // 8) * 8
    blocks = valid_blocks.shape[1]
    half = height // 2
    stride = half // n
    vmem = pl.BlockSpec(memory_space=pltpu.VMEM)
    encoded = pl.pallas_call(
        functools.partial(kernel, sizes),
        out_shape=jax.ShapeDtypeStruct((n - 1, stride, groups, 4 * OUTC), BF16),
        in_specs=[pl.BlockSpec(memory_space=pltpu.HBM)] * 7,
        out_specs=vmem,
        scratch_shapes=[
            pltpu.SMEM((n,), jnp.int32),
            pltpu.VMEM((height, lanes), BF16),
            pltpu.VMEM((blocks, groups), jnp.int32),
            pltpu.VMEM((CH, 9 * CH), BF16),
            pltpu.VMEM((1, CH), F32),
            pltpu.VMEM((OUTC, 27 * CH), BF16),
            pltpu.VMEM((1, OUTC), F32),
            pltpu.VMEM((3, (height + 6) * padded, 4 * CH), F32),
            pltpu.VMEM((2, 3, padded, 8 * CH), BF16),
            pltpu.VMEM((2, 3, padded, 8 * CH), BF16),
            pltpu.VMEM((9, height, 4 * CH), BF16),
            pltpu.VMEM((9, blocks, groups), jnp.int32),
            pltpu.VMEM((48 * CH, 8 * CH), BF16),
            pltpu.VMEM((24 * CH, 12 * OUTC), BF16),
            pltpu.VMEM((half + 2, padded, 4 * CH), BF16),
            pltpu.VMEM((n, stride + 2, padded, 4 * CH), BF16),
            pltpu.VMEM((n, stride, padded, 12 * OUTC), F32),
            pltpu.SemaphoreType.DMA((7,)),
            pltpu.SemaphoreType.DMA((9, 2)),
            pltpu.SemaphoreType.DMA((9, 2)),
            pltpu.SemaphoreType.DMA((n,)),
            pltpu.SemaphoreType.DMA((n,)),
        ],
        compiler_params=pltpu.CompilerParams(
            collective_id=0, has_side_effects=True, vmem_limit_bytes=64 * 1024 * 1024
        ),
    )(
        owner_map, raw, valid_blocks[0], deblock_weight.T, deblock_bias[None], encoder_weight.T,
        encoder_bias[None],
    )
    return encoded.reshape(n - 1, 1, stride, groups * 4 * OUTC)


def solution(mesh):
    sizes = (mesh.shape["tm"], mesh.shape["row"], mesh.shape["col"])
    return jax.shard_map(
        functools.partial(on_device, sizes),
        mesh=mesh,
        in_specs=(
            P(("grp", "tm"), "row", "col"),
            P("grp"),
            P(("grp", "tm"), "row", "col"),
            P(),
            P(),
            P(),
            P(),
        ),
        out_specs=P("grp", "row", "tm", "col"),
        check_vma=False,
    )
```

```python
import functools

import jax
import jax.numpy as jnp
from jax import lax
from jax.experimental import pallas as pl
from jax.experimental.pallas import tpu as pltpu
from jax.sharding import PartitionSpec as P

CH = 32
OUTC = 64
MESH = pl.DeviceIdType.MESH
F32 = jnp.float32
BF16 = jnp.bfloat16


def place(dr, dc):
    return (dr + 1) * 3 + dc + 1


DIRECTIONS = [(dr, dc) for dr in (-1, 0, 1) for dc in (-1, 0, 1) if (dr, dc) != (0, 0)]


def iota(shape, dim):
    return lax.broadcasted_iota(jnp.int32, shape, dim)


def spread_taps(taps, spread):
    return lax.dot_general(taps, spread, (((0,), (0,)), ((), ())), preferred_element_type=F32)


def deblock_matrix(dw_ref, t_ref):
    spread = (iota((CH, 4 * CH), 1) % CH == iota((CH, 4 * CH), 0)).astype(BF16)
    tiled = spread_taps(dw_ref[...], spread)
    taps = [[tiled[(3 * a + b) * CH : (3 * a + b + 1) * CH] for b in range(3)] for a in range(3)]
    wide = [
        [sum(row[b] for b in (d - 1, d) if 0 <= b < 3) for d in range(4)]
        for row in taps
    ]
    four = [
        [0.25 * sum(wide[a][d] for a in (e - 1, e) if 0 <= a < 3) for d in range(4)]
        for e in range(4)
    ]
    block = iota((CH, 4 * CH), 1) // CH
    zero = jnp.zeros((CH, 4 * CH), F32)
    rows, cols = iota((8 * CH, 4 * CH), 0), iota((8 * CH, 4 * CH), 1)
    mean = jnp.where((rows // (2 * CH) == cols // CH) & (rows % CH == cols % CH), 0.25, 0.0).astype(BF16)
    nothing = jnp.zeros((8 * CH, 4 * CH), BF16)
    for e in range(4):
        base = e * 12 * CH

        def put(at, pixel):
            total = zero
            for o in range(4):
                d = pixel - 2 * o + 1
                if 0 <= d < 4:
                    total = jnp.where(block == o, four[e][d], total)
            t_ref[base + at * CH : base + (at + 1) * CH, : 4 * CH] = total.astype(BF16)

        for pixel in range(8):
            put(pixel, pixel)
        put(8, 8)
        put(11, -1)
        t_ref[base + 9 * CH : base + 11 * CH, : 4 * CH] = nothing[: 2 * CH]
        t_ref[base : base + 8 * CH, 4 * CH :] = mean if e in (1, 2) else nothing
        t_ref[base + 8 * CH : base + 12 * CH, 4 * CH :] = nothing[: 4 * CH]


def encoder_matrix(ew_ref, t_ref):
    width = 4 * OUTC
    spread = (iota((OUTC, width), 1) % OUTC == iota((OUTC, width), 0)).astype(BF16)
    block = iota((CH, width), 1) // OUTC
    zero = jnp.zeros((CH, width), F32)
    nothing = jnp.zeros((2 * CH, width), BF16)
    everything = spread_taps(ew_ref[...], spread)
    for lag in range(3):
        tiled = everything[lag * 9 * CH : (lag + 1) * 9 * CH]
        for dy in range(3):
            base = dy * 8 * CH
            left = lag * width

            def put(at, pixel):
                total = zero
                for o in range(4):
                    d = pixel - o + 1
                    if 0 <= d < 3:
                        tap = tiled[(3 * dy + d) * CH : (3 * dy + d + 1) * CH]
                        total = jnp.where(block == o, tap, total)
                t_ref[base + at * CH : base + (at + 1) * CH, left : left + width] = total.astype(BF16)

            for pixel in range(4):
                put(pixel, pixel)
            put(4, 4)
            put(7, -1)
            t_ref[base + 5 * CH : base + 7 * CH, left : left + width] = nothing


def kernel(
    sizes,
    owner_hbm,
    raw_hbm,
    vb_hbm,
    dw_hbm,
    db_hbm,
    ew_hbm,
    eb_hbm,
    out_ref,
    owner_ref,
    raw_ref,
    vb_ref,
    dw_ref,
    db_ref,
    ew_ref,
    eb_ref,
    ext,
    outgoing,
    halo,
    edge,
    flags,
    tdeb,
    tenc,
    pooled,
    bands_in,
    product,
    lines,
    load_sem,
    send_sem,
    recv_sem,
    band_send,
    band_recv,
):
    n, nr, nc = sizes
    height, width = raw_ref.shape
    groups = width // (8 * CH)
    padded = halo.shape[2]
    half = height // 2
    stride = half // n
    me = lax.axis_index("tm")
    r = lax.axis_index("row")
    c = lax.axis_index("col")

    loads = [
        pltpu.make_async_copy(a, b, load_sem.at[k])
        for k, (a, b) in enumerate(
            (
                (raw_hbm, raw_ref),
                (vb_hbm, vb_ref),
                (dw_hbm, dw_ref),
                (db_hbm, db_ref),
                (ew_hbm, ew_ref),
                (eb_hbm, eb_ref),
                (owner_hbm, owner_ref),
            )
        )
    ]
    for load in loads:
        load.start()

    halo[...] = jnp.zeros_like(halo)
    edge[...] = jnp.zeros_like(edge)
    flags[...] = jnp.zeros_like(flags)

    def exists(dr, dc):
        found = None
        for step, at, count in ((dr, r, nr), (dc, c, nc)):
            if step:
                inside = at > 0 if step < 0 else at < count - 1
                found = inside if found is None else jnp.logical_and(found, inside)
        return found

    def copies(dr, dc):
        here, there = place(dr, dc), place(-dr, -dc)
        to = {}
        if dr:
            to["row"] = r + dr
        if dc:
            to["col"] = c + dc
        if dc:
            lanes = pl.ds(0, 4 * CH) if dc < 0 else pl.ds(raw_ref.shape[1] - 4 * CH, 4 * CH)
            src, dst = raw_ref.at[:, lanes], edge.at[there]
        else:
            src = outgoing.at[0 if dr < 0 else 1]
            dst = halo.at[1 if dr < 0 else 0]
        return [
            pltpu.make_async_remote_copy(
                src_ref=a, dst_ref=b, send_sem=send_sem.at[here, k], recv_sem=recv_sem.at[there, k],
                device_id=to, device_id_type=MESH,
            )
            for k, (a, b) in enumerate(((src, dst), (vb_ref, flags.at[there])))
        ]

    barrier = pltpu.get_barrier_semaphore()
    for dr, dc in DIRECTIONS:
        to = {}
        if dr:
            to["row"] = r + dr
        if dc:
            to["col"] = c + dc

        @pl.when(exists(dr, dc))
        def _():
            pl.semaphore_signal(barrier, inc=1, device_id=to, device_id_type=MESH)

    for d in range(1, n):
        pl.semaphore_signal(
            barrier, inc=1, device_id={"tm": lax.rem(me + d, n)}, device_id_type=MESH
        )
    ext[...] = jnp.zeros_like(ext)

    def line_of(k):
        return pl.ds(k * padded, padded)

    loads[0].wait()
    for h in range(0, height, 8):
        for q in range(2 * groups):
            ext[q % 2, pl.ds((3 + h) * padded + q // 2, 8, stride=padded), :] = raw_ref[
                h : h + 8, q * 4 * CH : (q + 1) * 4 * CH
            ].astype(F32)
    for side, dr in enumerate((-1, 1)):

        @pl.when(exists(dr, 0))
        def _():
            for k in range(3):
                line = line_of(3 + k if dr < 0 else height + k)
                for j in range(2):
                    outgoing[side, k, :, j * 4 * CH : (j + 1) * 4 * CH] = ext[j, line, :].astype(BF16)

    loads[1].wait()
    tall = (r > 0).astype(jnp.int32) + (r < nr - 1).astype(jnp.int32) + 1
    broad = (c > 0).astype(jnp.int32) + (c < nc - 1).astype(jnp.int32) + 1
    pl.semaphore_wait(barrier, tall * broad - 1 + n - 1)

    for dr, dc in DIRECTIONS:

        @pl.when(exists(dr, dc))
        def _():
            for copy in copies(dr, dc):
                copy.start()

    loads[2].wait()
    loads[3].wait()
    deblock_matrix(dw_ref, tdeb)

    for dr, dc in DIRECTIONS:

        @pl.when(exists(dr, dc))
        def _():
            for copy in copies(-dr, -dc):
                copy.wait_recv()

    for side, first in ((0, 0), (1, 3 + height)):
        for k in range(3):
            for j in range(2):
                ext[j, line_of(first + k), :] = halo[
                    side, k, :, j * 4 * CH : (j + 1) * 4 * CH
                ].astype(F32)
    for dc, at, j in ((-1, padded - 1, 1), (1, groups, 0)):
        for h in range(0, height, 8):
            ext[j, pl.ds((3 + h) * padded + at, 8, stride=padded), :] = edge[
                place(0, dc), h : h + 8
            ].astype(F32)
        top = edge[place(-1, dc)].astype(F32)
        low = edge[place(1, dc)].astype(F32)
        for k in range(3):
            for line, first in ((top[height - 3 + k : height - 2 + k], k), (low[k : k + 1], 3 + height + k)):
                ext[j, first * padded + at : first * padded + at + 1, :] = line

    lane = iota((padded, 4 * CH), 1)
    for k in range(height + 6):
        before = pltpu.roll(ext[1, line_of(k), :], 1, 0)
        after = pltpu.roll(ext[0, line_of(k), :], padded - 1, 0)
        ext[2, line_of(k), :] = jnp.where(
            lane >= 3 * CH, before, jnp.where(lane < CH, after, 0.0)
        )

    lhs = jnp.concatenate(
        [
            jnp.concatenate([ext[j, line_of(2 * k + e), :] for e in range(4) for j in range(3)], axis=1)
            for k in range(half + 2)
        ],
        axis=0,
    ).astype(BF16)
    conv = jnp.dot(lhs, tdeb[...], preferred_element_type=F32)

    def column(line, left, right):
        spot = iota((padded, groups), 0)
        own = jnp.sum(
            jnp.where(spot == iota((padded, groups), 1), jnp.broadcast_to(line, (padded, groups)), 0.0),
            axis=1, keepdims=True,
        )
        spot = iota((padded, 1), 0)
        own = jnp.where(spot == padded - 1, jnp.broadcast_to(left[:, groups - 1 :], (padded, 1)), own)
        return jnp.where(spot == groups, jnp.broadcast_to(right[:, :1], (padded, 1)), own)

    blocks = vb_ref.shape[0]

    def flag_row(dr, k):
        rows = [
            vb_ref[k : k + 1, :] if (dr, dc) == (0, 0) else flags[place(dr, dc), k : k + 1, :]
            for dc in (-1, 0, 1)
        ]
        left, line, right = [row.astype(F32) for row in rows]
        return column(line, left, right)

    masks = [flag_row(-1, blocks - 1)] + [flag_row(0, k) for k in range(blocks)] + [flag_row(1, 0)]
    deblock_bias = jnp.concatenate([db_ref[...]] * 4, axis=1)
    per = half // blocks
    for k in range(half + 2):
        part = conv[k * padded : (k + 1) * padded]
        which = 0 if k == 0 else blocks + 1 if k == half + 1 else 1 + (k - 1) // per
        pooled[k] = (
            part[:, 4 * CH :] + masks[which] * (part[:, : 4 * CH] + deblock_bias)
        ).astype(BF16)

    def band_copy(to):
        return pltpu.make_async_remote_copy(
            src_ref=pooled.at[pl.ds(to * stride, stride + 2)],
            dst_ref=bands_in.at[me],
            send_sem=band_send.at[to],
            recv_sem=band_recv.at[me],
            device_id={"tm": to},
            device_id_type=MESH,
        )

    def band_arrival(source):
        return pltpu.make_async_remote_copy(
            src_ref=pooled.at[pl.ds(0, stride + 2)],
            dst_ref=bands_in.at[source],
            send_sem=band_send.at[source],
            recv_sem=band_recv.at[source],
            device_id={"tm": source},
            device_id_type=MESH,
        )

    first, last = jnp.int32(0), jnp.int32(n - 1)
    for _ in range(n - 1):
        down = me - first > last - me
        to = jnp.where(down, first, last)
        band_copy(to).start()
        first, last = jnp.where(down, first + 1, first), jnp.where(down, last, last - 1)
    bands_in[me] = pooled[pl.ds(me * stride, stride + 2)]
    loads[4].wait()
    encoder_matrix(ew_ref, tenc)
    loads[5].wait()
    loads[6].wait()
    for d in range(1, n):
        band_arrival(lax.rem(me + d, n)).wait_recv()

    rows = []
    for s in range(n):
        shifted = []
        for k in range(stride + 2):
            own = bands_in[s, k].astype(F32)
            side = jnp.where(
                lane >= 3 * CH,
                pltpu.roll(own, 1, 0),
                jnp.where(lane < CH, pltpu.roll(own, padded - 1, 0), 0.0),
            )
            shifted.append(jnp.concatenate([own, side], axis=1))
        for k in range(stride):
            rows.append(jnp.concatenate(shifted[k : k + 3], axis=1))
    lhs = jnp.concatenate(rows, axis=0).astype(BF16)
    found = jnp.dot(lhs, tenc[...], preferred_element_type=F32)
    product[...] = found.reshape(product.shape)

    slots = []
    for t in range(n):
        if n <= 8:
            slot = jnp.int32(0)
            for s in range(n):
                slot = jnp.where(owner_ref[s] == t, s, slot)
        else:
            slot = lax.fori_loop(
                0, n, lambda s, held: jnp.where(owner_ref[s] == t, s, held), jnp.int32(0)
            )
        slots.append(slot)
    width = 4 * OUTC
    encoder_bias = jnp.concatenate([eb_ref[...]] * 4, axis=1)
    for t in range(1, n):
        for k in range(stride):
            total = encoder_bias
            for lag in range(3):
                total = total + product[slots[max(t - lag, 0)], k, :, lag * width : (lag + 1) * width]
            for j in range(2):
                lines[j, line_of((t - 1) * stride + k), :] = total[:, j * 4 * CH : (j + 1) * 4 * CH]
    for h in range(0, (n - 1) * stride, 8):
        count = min(8, (n - 1) * stride - h)
        for q in range(2 * groups):
            out_ref[h : h + count, q * 4 * CH : (q + 1) * 4 * CH] = lines[
                q % 2, pl.ds(h * padded + q // 2, count, stride=padded), :
            ].astype(BF16)

    for dr, dc in DIRECTIONS:

        @pl.when(exists(dr, dc))
        def _():
            for copy in copies(dr, dc):
                copy.wait_send()

    for d in range(1, n):
        band_copy(lax.rem(me + d, n)).wait_send()


def on_device(
    sizes, frames, owner_map, valid_blocks, deblock_weight, deblock_bias, encoder_weight, encoder_bias
):
    n = sizes[0]
    _, height, lanes = frames.shape
    raw = frames[0]
    groups = lanes // (8 * CH)
    padded = -(-(groups + 2) // 8) * 8
    blocks = valid_blocks.shape[1]
    half = height // 2
    stride = half // n
    vmem = pl.BlockSpec(memory_space=pltpu.VMEM)
    operands = (
        owner_map, raw, valid_blocks[0], deblock_weight.T, deblock_bias[None], encoder_weight.T,
        encoder_bias[None],
    )
    encoded = pl.pallas_call(
        functools.partial(kernel, sizes),
        out_shape=jax.ShapeDtypeStruct(((n - 1) * stride, groups * 4 * OUTC), BF16),
        in_specs=[pl.BlockSpec(memory_space=pltpu.HBM)] * 7,
        out_specs=vmem,
        scratch_shapes=[
            pltpu.SMEM((n,), jnp.int32),
            pltpu.VMEM((height, lanes), BF16),
            pltpu.VMEM((blocks, groups), jnp.int32),
            pltpu.VMEM((CH, 9 * CH), BF16),
            pltpu.VMEM((1, CH), F32),
            pltpu.VMEM((OUTC, 27 * CH), BF16),
            pltpu.VMEM((1, OUTC), F32),
            pltpu.VMEM((3, (height + 6) * padded, 4 * CH), F32),
            pltpu.VMEM((2, 3, padded, 8 * CH), BF16),
            pltpu.VMEM((2, 3, padded, 8 * CH), BF16),
            pltpu.VMEM((9, height, 4 * CH), BF16),
            pltpu.VMEM((9, blocks, groups), jnp.int32),
            pltpu.VMEM((48 * CH, 8 * CH), BF16),
            pltpu.VMEM((24 * CH, 12 * OUTC), BF16),
            pltpu.VMEM((half + 2, padded, 4 * CH), BF16),
            pltpu.VMEM((n, stride + 2, padded, 4 * CH), BF16),
            pltpu.VMEM((n, stride, padded, 12 * OUTC), F32),
            pltpu.VMEM((2, (n - 1) * stride * padded, 4 * CH), F32),
            pltpu.SemaphoreType.DMA((7,)),
            pltpu.SemaphoreType.DMA((9, 2)),
            pltpu.SemaphoreType.DMA((9, 2)),
            pltpu.SemaphoreType.DMA((n,)),
            pltpu.SemaphoreType.DMA((n,)),
        ],
        compiler_params=pltpu.CompilerParams(
            collective_id=0, has_side_effects=True, vmem_limit_bytes=40 * 1024 * 1024
        ),
    )(*[pltpu.with_memory_space_constraint(operand, pltpu.HBM) for operand in operands])
    return encoded.reshape(n - 1, 1, stride, groups * 4 * OUTC)


def solution(mesh):
    sizes = (mesh.shape["tm"], mesh.shape["row"], mesh.shape["col"])
    return jax.shard_map(
        functools.partial(on_device, sizes),
        mesh=mesh,
        in_specs=(
            P(("grp", "tm"), "row", "col"),
            P("grp"),
            P(("grp", "tm"), "row", "col"),
            P(),
            P(),
            P(),
            P(),
        ),
        out_specs=P("grp", "row", "tm", "col"),
        check_vma=False,
    )
```

```python
import functools

import jax
import jax.numpy as jnp
from jax import lax
from jax.experimental import pallas as pl
from jax.experimental.pallas import tpu as pltpu
from jax.sharding import PartitionSpec as P

CH = 32
OUTC = 64
MESH = pl.DeviceIdType.MESH
F32 = jnp.float32
BF16 = jnp.bfloat16


def place(dr, dc):
    return (dr + 1) * 3 + dc + 1


DIRECTIONS = [(dr, dc) for dr in (-1, 0, 1) for dc in (-1, 0, 1) if (dr, dc) != (0, 0)]


def iota(shape, dim):
    return lax.broadcasted_iota(jnp.int32, shape, dim)


def spread_taps(taps, spread):
    return lax.dot_general(taps, spread, (((0,), (0,)), ((), ())), preferred_element_type=F32)


def deblock_matrix(dw_ref, t_ref):
    spread = (iota((CH, 4 * CH), 1) % CH == iota((CH, 4 * CH), 0)).astype(BF16)
    tiled = spread_taps(dw_ref[...], spread)
    taps = [[tiled[(3 * a + b) * CH : (3 * a + b + 1) * CH] for b in range(3)] for a in range(3)]
    wide = [
        [sum(row[b] for b in (d - 1, d) if 0 <= b < 3) for d in range(4)]
        for row in taps
    ]
    four = [
        [0.25 * sum(wide[a][d] for a in (e - 1, e) if 0 <= a < 3) for d in range(4)]
        for e in range(4)
    ]
    block = iota((CH, 4 * CH), 1) // CH
    zero = jnp.zeros((CH, 4 * CH), F32)
    rows, cols = iota((8 * CH, 4 * CH), 0), iota((8 * CH, 4 * CH), 1)
    mean = jnp.where((rows // (2 * CH) == cols // CH) & (rows % CH == cols % CH), 0.25, 0.0).astype(BF16)
    nothing = jnp.zeros((8 * CH, 4 * CH), BF16)
    for e in range(4):
        base = e * 12 * CH

        def put(at, pixel):
            total = zero
            for o in range(4):
                d = pixel - 2 * o + 1
                if 0 <= d < 4:
                    total = jnp.where(block == o, four[e][d], total)
            t_ref[base + at * CH : base + (at + 1) * CH, : 4 * CH] = total.astype(BF16)

        for pixel in range(8):
            put(pixel, pixel)
        put(8, 8)
        put(11, -1)
        t_ref[base + 9 * CH : base + 11 * CH, : 4 * CH] = nothing[: 2 * CH]
        t_ref[base : base + 8 * CH, 4 * CH :] = mean if e in (1, 2) else nothing
        t_ref[base + 8 * CH : base + 12 * CH, 4 * CH :] = nothing[: 4 * CH]


def encoder_matrix(ew_ref, t_ref):
    width = 4 * OUTC
    spread = (iota((OUTC, width), 1) % OUTC == iota((OUTC, width), 0)).astype(BF16)
    block = iota((CH, width), 1) // OUTC
    zero = jnp.zeros((CH, width), F32)
    nothing = jnp.zeros((2 * CH, width), BF16)
    everything = spread_taps(ew_ref[...], spread)
    for lag in range(3):
        tiled = everything[lag * 9 * CH : (lag + 1) * 9 * CH]
        for dy in range(3):
            base = dy * 8 * CH
            left = lag * width

            def put(at, pixel):
                total = zero
                for o in range(4):
                    d = pixel - o + 1
                    if 0 <= d < 3:
                        tap = tiled[(3 * dy + d) * CH : (3 * dy + d + 1) * CH]
                        total = jnp.where(block == o, tap, total)
                t_ref[base + at * CH : base + (at + 1) * CH, left : left + width] = total.astype(BF16)

            for pixel in range(4):
                put(pixel, pixel)
            put(4, 4)
            put(7, -1)
            t_ref[base + 5 * CH : base + 7 * CH, left : left + width] = nothing


def kernel(
    sizes,
    owner_hbm,
    raw_hbm,
    vb_hbm,
    dw_hbm,
    db_hbm,
    ew_hbm,
    eb_hbm,
    out_ref,
    owner_ref,
    raw_ref,
    vb_ref,
    dw_ref,
    db_ref,
    ew_ref,
    eb_ref,
    ext,
    edge,
    flags,
    tdeb,
    tenc,
    pooled,
    bands_in,
    beside,
    product,
    lines,
    load_sem,
    send_sem,
    recv_sem,
    band_send,
    band_recv,
    beside_send,
    beside_recv,
):
    n, nr, nc = sizes
    height, width = raw_ref.shape
    groups = width // (8 * CH)
    padded = pooled.shape[1]
    half = height // 2
    stride = half // n
    me = lax.axis_index("tm")
    r = lax.axis_index("row")
    c = lax.axis_index("col")

    loads = [
        pltpu.make_async_copy(a, b, load_sem.at[k])
        for k, (a, b) in enumerate(
            (
                (raw_hbm, raw_ref),
                (vb_hbm, vb_ref),
                (dw_hbm, dw_ref),
                (db_hbm, db_ref),
                (ew_hbm, ew_ref),
                (eb_hbm, eb_ref),
                (owner_hbm, owner_ref),
            )
        )
    ]
    for load in loads:
        load.start()

    edge[...] = jnp.zeros_like(edge)
    flags[...] = jnp.zeros_like(flags)
    beside[...] = jnp.zeros_like(beside)

    def exists(dr, dc):
        found = None
        for step, at, count in ((dr, r, nr), (dc, c, nc)):
            if step:
                inside = at > 0 if step < 0 else at < count - 1
                found = inside if found is None else jnp.logical_and(found, inside)
        return found

    def copies(dr, dc):
        here, there = place(dr, dc), place(-dr, -dc)
        to = {}
        if dr:
            to["row"] = r + dr
        if dc:
            to["col"] = c + dc
        pairs = [(vb_hbm, flags.at[there])]
        if not dr:
            lanes = pl.ds(0 if dc < 0 else width - 4 * CH, 4 * CH)
            pairs.append((raw_hbm.at[:, lanes], edge.at[(1 - dc) // 2]))
        return [
            pltpu.make_async_remote_copy(
                src_ref=a, dst_ref=b, send_sem=send_sem.at[here, k], recv_sem=recv_sem.at[there, k],
                device_id=to, device_id_type=MESH,
            )
            for k, (a, b) in enumerate(pairs)
        ]

    barrier = pltpu.get_barrier_semaphore()
    for dr, dc in DIRECTIONS:
        if not dc:
            continue
        to = {"col": c + dc}
        if dr:
            to["row"] = r + dr

        @pl.when(exists(dr, dc))
        def _():
            pl.semaphore_signal(barrier, inc=1, device_id=to, device_id_type=MESH)

    for d in range(1, n):
        pl.semaphore_signal(
            barrier, inc=1, device_id={"tm": lax.rem(me + d, n)}, device_id_type=MESH
        )
    for dr in (-1, 1):

        @pl.when(exists(dr, 0))
        def _():
            for t in range(n):
                pl.semaphore_signal(
                    barrier, inc=1, device_id={"tm": t, "row": r + dr}, device_id_type=MESH
                )

    tall = (r > 0).astype(jnp.int32) + (r < nr - 1).astype(jnp.int32) + 1
    broad = (c > 0).astype(jnp.int32) + (c < nc - 1).astype(jnp.int32)
    pl.semaphore_wait(barrier, tall * broad + tall * n - 1)

    for dr, dc in sorted(DIRECTIONS, key=lambda item: item[0] != 0):

        @pl.when(exists(dr, dc))
        def _():
            for copy in reversed(copies(dr, dc)):
                copy.start()

    ext[...] = jnp.zeros_like(ext)

    def line_of(k):
        return pl.ds(k * padded, padded)

    loads[0].wait()
    for h in range(0, height, 8):
        for q in range(2 * groups):
            ext[q % 2, pl.ds(h * padded + q // 2, 8, stride=padded), :] = raw_ref[
                h : h + 8, q * 4 * CH : (q + 1) * 4 * CH
            ].astype(F32)

    loads[1].wait()
    loads[2].wait()
    loads[3].wait()
    deblock_matrix(dw_ref, tdeb)

    for dr, dc in DIRECTIONS:

        @pl.when(exists(dr, dc))
        def _():
            for copy in copies(-dr, -dc):
                copy.wait_recv()

    for side, at, j in ((0, padded - 1, 1), (1, groups, 0)):
        for h in range(0, height, 8):
            ext[j, pl.ds(h * padded + at, 8, stride=padded), :] = edge[side, h : h + 8].astype(F32)

    lane = iota((padded, 4 * CH), 1)
    for k in range(height):
        before = pltpu.roll(ext[1, line_of(k), :], 1, 0)
        after = pltpu.roll(ext[0, line_of(k), :], padded - 1, 0)
        ext[2, line_of(k), :] = jnp.where(
            lane >= 3 * CH, before, jnp.where(lane < CH, after, 0.0)
        )

    nothing = jnp.zeros((padded, 4 * CH), F32)
    lhs = jnp.concatenate(
        [
            jnp.concatenate(
                [
                    ext[j, line_of(2 * k + e - 3), :] if 0 <= 2 * k + e - 3 < height else nothing
                    for e in range(4)
                    for j in range(3)
                ],
                axis=1,
            )
            for k in range(half + 2)
        ],
        axis=0,
    ).astype(BF16)
    conv = jnp.dot(lhs, tdeb[...], preferred_element_type=F32)

    def column(line, left, right):
        spot = iota((padded, groups), 0)
        own = jnp.sum(
            jnp.where(spot == iota((padded, groups), 1), jnp.broadcast_to(line, (padded, groups)), 0.0),
            axis=1, keepdims=True,
        )
        spot = iota((padded, 1), 0)
        own = jnp.where(spot == padded - 1, jnp.broadcast_to(left[:, groups - 1 :], (padded, 1)), own)
        return jnp.where(spot == groups, jnp.broadcast_to(right[:, :1], (padded, 1)), own)

    blocks = vb_ref.shape[0]

    def flag_row(dr, k):
        rows = [
            vb_ref[k : k + 1, :] if (dr, dc) == (0, 0) else flags[place(dr, dc), k : k + 1, :]
            for dc in (-1, 0, 1)
        ]
        left, line, right = [row.astype(F32) for row in rows]
        return column(line, left, right)

    masks = [flag_row(-1, blocks - 1)] + [flag_row(0, k) for k in range(blocks)] + [flag_row(1, 0)]
    deblock_bias = jnp.concatenate([db_ref[...]] * 4, axis=1)
    per = half // blocks
    for k in range(half + 2):
        part = conv[k * padded : (k + 1) * padded]
        which = 0 if k == 0 else blocks + 1 if k == half + 1 else 1 + (k - 1) // per
        term = part[:, : 4 * CH]
        if 1 <= k <= half:
            term = term + deblock_bias
        pooled[k] = (part[:, 4 * CH :] + masks[which] * term).astype(BF16)

    def band_copy(to):
        return pltpu.make_async_remote_copy(
            src_ref=pooled.at[pl.ds(to * stride, stride + 2)],
            dst_ref=bands_in.at[me],
            send_sem=band_send.at[to],
            recv_sem=band_recv.at[me],
            device_id={"tm": to},
            device_id_type=MESH,
        )

    def band_arrival(source):
        return pltpu.make_async_remote_copy(
            src_ref=pooled.at[pl.ds(0, stride + 2)],
            dst_ref=bands_in.at[source],
            send_sem=band_send.at[source],
            recv_sem=band_recv.at[source],
            device_id={"tm": source},
            device_id_type=MESH,
        )

    spreads = []
    for side, dr in enumerate((1, -1)):
        for gap in range(2 if stride == 1 else 1):
            band = gap if dr > 0 else n - 1 - gap
            source = half + gap if dr > 0 else 0
            target = 0 if dr > 0 else stride + gap
            spreads.append((side, dr, gap, band, pl.ds(source, 2 - gap), pl.ds(target, 2 - gap)))

    def beside_copy(item, frame):
        side, dr, gap, band, source, target = item
        return pltpu.make_async_remote_copy(
            src_ref=pooled.at[source],
            dst_ref=beside.at[side, frame, target],
            send_sem=beside_send.at[side, gap],
            recv_sem=beside_recv.at[side, frame],
            device_id={"tm": band, "row": r + dr},
            device_id_type=MESH,
        )

    for item in spreads:

        @pl.when(exists(item[1], 0))
        def _():
            beside_copy(item, me).start()

    first, last = jnp.int32(0), jnp.int32(n - 1)
    for _ in range(n - 1):
        down = me - first > last - me
        to = jnp.where(down, first, last)
        band_copy(to).start()
        first, last = jnp.where(down, first + 1, first), jnp.where(down, last, last - 1)
    bands_in[me] = pooled[pl.ds(me * stride, stride + 2)]
    loads[4].wait()
    encoder_matrix(ew_ref, tenc)
    loads[5].wait()
    loads[6].wait()
    for d in range(1, n):
        band_arrival(lax.rem(me + d, n)).wait_recv()
    for item in spreads:

        @pl.when(jnp.logical_and(exists(-item[1], 0), me == item[3]))
        def _():
            for frame in range(n):
                beside_copy(item, frame).wait_recv()

    rows = []
    for s in range(n):
        shifted = []
        for k in range(stride + 2):
            own = bands_in[s, k].astype(F32) + beside[0, s, k].astype(F32) + beside[1, s, k].astype(F32)
            side = jnp.where(
                lane >= 3 * CH,
                pltpu.roll(own, 1, 0),
                jnp.where(lane < CH, pltpu.roll(own, padded - 1, 0), 0.0),
            )
            shifted.append(jnp.concatenate([own, side], axis=1))
        for k in range(stride):
            rows.append(jnp.concatenate(shifted[k : k + 3], axis=1))
    lhs = jnp.concatenate(rows, axis=0).astype(BF16)
    found = jnp.dot(lhs, tenc[...], preferred_element_type=F32)
    product[...] = found.reshape(product.shape)

    slots = []
    for t in range(n):
        if n <= 8:
            slot = jnp.int32(0)
            for s in range(n):
                slot = jnp.where(owner_ref[s] == t, s, slot)
        else:
            slot = lax.fori_loop(
                0, n, lambda s, held: jnp.where(owner_ref[s] == t, s, held), jnp.int32(0)
            )
        slots.append(slot)
    width = 4 * OUTC
    encoder_bias = jnp.concatenate([eb_ref[...]] * 4, axis=1)
    for t in range(1, n):
        for k in range(stride):
            total = encoder_bias
            for lag in range(3):
                total = total + product[slots[max(t - lag, 0)], k, :, lag * width : (lag + 1) * width]
            for j in range(2):
                lines[j, line_of((t - 1) * stride + k), :] = total[:, j * 4 * CH : (j + 1) * 4 * CH]
    for h in range(0, (n - 1) * stride, 8):
        count = min(8, (n - 1) * stride - h)
        for q in range(2 * groups):
            out_ref[h : h + count, q * 4 * CH : (q + 1) * 4 * CH] = lines[
                q % 2, pl.ds(h * padded + q // 2, count, stride=padded), :
            ].astype(BF16)

    for dr, dc in DIRECTIONS:

        @pl.when(exists(dr, dc))
        def _():
            for copy in copies(dr, dc):
                copy.wait_send()

    for d in range(1, n):
        band_copy(lax.rem(me + d, n)).wait_send()

    for item in spreads:

        @pl.when(exists(item[1], 0))
        def _():
            beside_copy(item, me).wait_send()


def on_device(
    sizes, frames, owner_map, valid_blocks, deblock_weight, deblock_bias, encoder_weight, encoder_bias
):
    n = sizes[0]
    _, height, lanes = frames.shape
    raw = frames[0]
    groups = lanes // (8 * CH)
    padded = -(-(groups + 2) // 8) * 8
    blocks = valid_blocks.shape[1]
    half = height // 2
    stride = half // n
    vmem = pl.BlockSpec(memory_space=pltpu.VMEM)
    operands = (
        owner_map, raw, valid_blocks[0], deblock_weight.T, deblock_bias[None], encoder_weight.T,
        encoder_bias[None],
    )
    encoded = pl.pallas_call(
        functools.partial(kernel, sizes),
        out_shape=jax.ShapeDtypeStruct(((n - 1) * stride, groups * 4 * OUTC), BF16),
        in_specs=[pl.BlockSpec(memory_space=pltpu.HBM)] * 7,
        out_specs=vmem,
        scratch_shapes=[
            pltpu.SMEM((n,), jnp.int32),
            pltpu.VMEM((height, lanes), BF16),
            pltpu.VMEM((blocks, groups), jnp.int32),
            pltpu.VMEM((CH, 9 * CH), BF16),
            pltpu.VMEM((1, CH), F32),
            pltpu.VMEM((OUTC, 27 * CH), BF16),
            pltpu.VMEM((1, OUTC), F32),
            pltpu.VMEM((3, height * padded, 4 * CH), F32),
            pltpu.VMEM((2, height, 4 * CH), BF16),
            pltpu.VMEM((9, blocks, groups), jnp.int32),
            pltpu.VMEM((48 * CH, 8 * CH), BF16),
            pltpu.VMEM((24 * CH, 12 * OUTC), BF16),
            pltpu.VMEM((half + 2, padded, 4 * CH), BF16),
            pltpu.VMEM((n, stride + 2, padded, 4 * CH), BF16),
            pltpu.VMEM((2, n, stride + 2, padded, 4 * CH), BF16),
            pltpu.VMEM((n, stride, padded, 12 * OUTC), F32),
            pltpu.VMEM((2, (n - 1) * stride * padded, 4 * CH), F32),
            pltpu.SemaphoreType.DMA((7,)),
            pltpu.SemaphoreType.DMA((9, 2)),
            pltpu.SemaphoreType.DMA((9, 2)),
            pltpu.SemaphoreType.DMA((n,)),
            pltpu.SemaphoreType.DMA((n,)),
            pltpu.SemaphoreType.DMA((2, 2)),
            pltpu.SemaphoreType.DMA((2, n)),
        ],
        compiler_params=pltpu.CompilerParams(
            collective_id=0, has_side_effects=True, vmem_limit_bytes=40 * 1024 * 1024
        ),
    )(*[pltpu.with_memory_space_constraint(operand, pltpu.HBM) for operand in operands])
    return encoded.reshape(n - 1, 1, stride, groups * 4 * OUTC)


def solution(mesh):
    sizes = (mesh.shape["tm"], mesh.shape["row"], mesh.shape["col"])
    return jax.shard_map(
        functools.partial(on_device, sizes),
        mesh=mesh,
        in_specs=(
            P(("grp", "tm"), "row", "col"),
            P("grp"),
            P(("grp", "tm"), "row", "col"),
            P(),
            P(),
            P(),
            P(),
        ),
        out_specs=P("grp", "row", "tm", "col"),
        check_vma=False,
    )
```

```python
import functools

import jax
import jax.numpy as jnp
from jax import lax
from jax.experimental import pallas as pl
from jax.experimental.pallas import tpu as pltpu
from jax.sharding import PartitionSpec as P

CH = 32
OUTC = 64
MESH = pl.DeviceIdType.MESH
F32 = jnp.float32
BF16 = jnp.bfloat16


def place(dr, dc):
    return (dr + 1) * 3 + dc + 1


DIRECTIONS = [(dr, dc) for dr in (-1, 0, 1) for dc in (-1, 0, 1) if (dr, dc) != (0, 0)]


def iota(shape, dim):
    return lax.broadcasted_iota(jnp.int32, shape, dim)


def spread_taps(taps, spread):
    return lax.dot_general(taps, spread, (((0,), (0,)), ((), ())), preferred_element_type=F32)


def deblock_matrix(dw_ref, t_ref):
    spread = (iota((CH, 4 * CH), 1) % CH == iota((CH, 4 * CH), 0)).astype(BF16)
    tiled = spread_taps(dw_ref[...], spread)
    taps = [[tiled[(3 * a + b) * CH : (3 * a + b + 1) * CH] for b in range(3)] for a in range(3)]
    wide = [
        [sum(row[b] for b in (d - 1, d) if 0 <= b < 3) for d in range(4)]
        for row in taps
    ]
    four = [
        [0.25 * sum(wide[a][d] for a in (e - 1, e) if 0 <= a < 3) for d in range(4)]
        for e in range(4)
    ]
    block = iota((CH, 4 * CH), 1) // CH
    zero = jnp.zeros((CH, 4 * CH), F32)
    rows, cols = iota((8 * CH, 4 * CH), 0), iota((8 * CH, 4 * CH), 1)
    mean = jnp.where((rows // (2 * CH) == cols // CH) & (rows % CH == cols % CH), 0.25, 0.0).astype(BF16)
    nothing = jnp.zeros((8 * CH, 4 * CH), BF16)
    for e in range(4):
        base = e * 12 * CH

        def put(at, pixel):
            total = zero
            for o in range(4):
                d = pixel - 2 * o + 1
                if 0 <= d < 4:
                    total = jnp.where(block == o, four[e][d], total)
            t_ref[base + at * CH : base + (at + 1) * CH, : 4 * CH] = total.astype(BF16)

        for pixel in range(8):
            put(pixel, pixel)
        put(8, 8)
        put(11, -1)
        t_ref[base + 9 * CH : base + 11 * CH, : 4 * CH] = nothing[: 2 * CH]
        t_ref[base : base + 8 * CH, 4 * CH :] = mean if e in (1, 2) else nothing
        t_ref[base + 8 * CH : base + 12 * CH, 4 * CH :] = nothing[: 4 * CH]


def encoder_matrix(ew_ref, t_ref):
    width = 4 * OUTC
    spread = (iota((OUTC, width), 1) % OUTC == iota((OUTC, width), 0)).astype(BF16)
    block = iota((CH, width), 1) // OUTC
    zero = jnp.zeros((CH, width), F32)
    nothing = jnp.zeros((2 * CH, width), BF16)
    everything = spread_taps(ew_ref[...], spread)
    for lag in range(3):
        tiled = everything[lag * 9 * CH : (lag + 1) * 9 * CH]
        for dy in range(3):
            base = dy * 8 * CH
            left = lag * width

            def put(at, pixel):
                total = zero
                for o in range(4):
                    d = pixel - o + 1
                    if 0 <= d < 3:
                        tap = tiled[(3 * dy + d) * CH : (3 * dy + d + 1) * CH]
                        total = jnp.where(block == o, tap, total)
                t_ref[base + at * CH : base + (at + 1) * CH, left : left + width] = total.astype(BF16)

            for pixel in range(4):
                put(pixel, pixel)
            put(4, 4)
            put(7, -1)
            t_ref[base + 5 * CH : base + 7 * CH, left : left + width] = nothing


def kernel(
    sizes,
    owner_hbm,
    raw_hbm,
    vb_hbm,
    dw_hbm,
    db_hbm,
    ew_hbm,
    eb_hbm,
    out_ref,
    owner_ref,
    raw_ref,
    vb_ref,
    dw_ref,
    db_ref,
    ew_ref,
    eb_ref,
    ext,
    outgoing,
    halo,
    edge,
    flags,
    tdeb,
    tenc,
    pooled,
    bands_in,
    product,
    lines,
    load_sem,
    send_sem,
    recv_sem,
    band_send,
    band_recv,
):
    n, nr, nc = sizes
    height, width = raw_ref.shape
    groups = width // (8 * CH)
    padded = halo.shape[2]
    half = height // 2
    stride = half // n
    me = lax.axis_index("tm")
    r = lax.axis_index("row")
    c = lax.axis_index("col")

    loads = [
        pltpu.make_async_copy(a, b, load_sem.at[k])
        for k, (a, b) in enumerate(
            (
                (raw_hbm, raw_ref),
                (vb_hbm, vb_ref),
                (dw_hbm, dw_ref),
                (db_hbm, db_ref),
                (ew_hbm, ew_ref),
                (eb_hbm, eb_ref),
                (owner_hbm, owner_ref),
            )
        )
    ]
    for load in loads:
        load.start()

    halo[...] = jnp.zeros_like(halo)
    edge[...] = jnp.zeros_like(edge)
    flags[...] = jnp.zeros_like(flags)

    def exists(dr, dc):
        found = None
        for step, at, count in ((dr, r, nr), (dc, c, nc)):
            if step:
                inside = at > 0 if step < 0 else at < count - 1
                found = inside if found is None else jnp.logical_and(found, inside)
        return found

    def copies(dr, dc):
        here, there = place(dr, dc), place(-dr, -dc)
        to = {}
        if dr:
            to["row"] = r + dr
        if dc:
            to["col"] = c + dc
        if dc:
            lanes = pl.ds(0, 4 * CH) if dc < 0 else pl.ds(raw_ref.shape[1] - 4 * CH, 4 * CH)
            src, dst = raw_ref.at[:, lanes], edge.at[there]
        else:
            src = outgoing.at[0 if dr < 0 else 1]
            dst = halo.at[1 if dr < 0 else 0]
        return [
            pltpu.make_async_remote_copy(
                src_ref=a, dst_ref=b, send_sem=send_sem.at[here, k], recv_sem=recv_sem.at[there, k],
                device_id=to, device_id_type=MESH,
            )
            for k, (a, b) in enumerate(((src, dst), (vb_ref, flags.at[there])))
        ]

    barrier = pltpu.get_barrier_semaphore()
    for dr, dc in DIRECTIONS:
        to = {}
        if dr:
            to["row"] = r + dr
        if dc:
            to["col"] = c + dc

        @pl.when(exists(dr, dc))
        def _():
            pl.semaphore_signal(barrier, inc=1, device_id=to, device_id_type=MESH)

    for d in range(1, n):
        pl.semaphore_signal(
            barrier, inc=1, device_id={"tm": lax.rem(me + d, n)}, device_id_type=MESH
        )
    ext[...] = jnp.zeros_like(ext)

    def line_of(k):
        return pl.ds(k * padded, padded)

    loads[0].wait()
    for h in range(0, height, 8):
        for q in range(2 * groups):
            ext[q % 2, pl.ds((3 + h) * padded + q // 2, 8, stride=padded), :] = raw_ref[
                h : h + 8, q * 4 * CH : (q + 1) * 4 * CH
            ].astype(F32)
    for side, dr in enumerate((-1, 1)):

        @pl.when(exists(dr, 0))
        def _():
            for k in range(3):
                line = line_of(3 + k if dr < 0 else height + k)
                for j in range(2):
                    outgoing[side, k, :, j * 4 * CH : (j + 1) * 4 * CH] = ext[j, line, :].astype(BF16)

    loads[1].wait()
    tall = (r > 0).astype(jnp.int32) + (r < nr - 1).astype(jnp.int32) + 1
    broad = (c > 0).astype(jnp.int32) + (c < nc - 1).astype(jnp.int32) + 1
    pl.semaphore_wait(barrier, tall * broad - 1 + n - 1)

    for dr, dc in DIRECTIONS:

        @pl.when(exists(dr, dc))
        def _():
            for copy in copies(dr, dc):
                copy.start()

    lanes_of = iota((padded, 4 * CH), 1)

    def beside(k):
        before = pltpu.roll(ext[1, line_of(k), :], 1, 0)
        after = pltpu.roll(ext[0, line_of(k), :], padded - 1, 0)
        ext[2, line_of(k), :] = jnp.where(
            lanes_of >= 3 * CH, before, jnp.where(lanes_of < CH, after, 0.0)
        )

    for k in range(3, 3 + height):
        beside(k)
    loads[2].wait()
    loads[3].wait()
    deblock_matrix(dw_ref, tdeb)

    for dr, dc in DIRECTIONS:

        @pl.when(exists(dr, dc))
        def _():
            for copy in copies(-dr, -dc):
                copy.wait_recv()

    for side, first in ((0, 0), (1, 3 + height)):
        for k in range(3):
            for j in range(2):
                ext[j, line_of(first + k), :] = halo[
                    side, k, :, j * 4 * CH : (j + 1) * 4 * CH
                ].astype(F32)
    for dc, at, j in ((-1, padded - 1, 1), (1, groups, 0)):
        for h in range(0, height, 8):
            ext[j, pl.ds((3 + h) * padded + at, 8, stride=padded), :] = edge[
                place(0, dc), h : h + 8
            ].astype(F32)
        top = edge[place(-1, dc)].astype(F32)
        low = edge[place(1, dc)].astype(F32)
        for k in range(3):
            for line, first in ((top[height - 3 + k : height - 2 + k], k), (low[k : k + 1], 3 + height + k)):
                ext[j, first * padded + at : first * padded + at + 1, :] = line

    for k in (0, 1, 2, height + 3, height + 4, height + 5):
        beside(k)
    lane = iota((8, 4 * CH), 1)
    for h in range(0, height, 8):
        for side, at, j in ((0, 0, padded - 1), (1, groups - 1, groups)):
            spot = pl.ds((3 + h) * padded + at, 8, stride=padded)
            chosen = lane >= 3 * CH if side == 0 else lane < CH
            came = edge[place(0, -1 if side == 0 else 1), h : h + 8].astype(F32)
            ext[2, spot, :] = jnp.where(chosen, came, ext[2, spot, :])

    lhs = jnp.concatenate(
        [
            jnp.concatenate([ext[j, line_of(2 * k + e), :] for e in range(4) for j in range(3)], axis=1)
            for k in range(half + 2)
        ],
        axis=0,
    ).astype(BF16)
    conv = jnp.dot(lhs, tdeb[...], preferred_element_type=F32)

    def column(line, left, right):
        spot = iota((padded, groups), 0)
        own = jnp.sum(
            jnp.where(spot == iota((padded, groups), 1), jnp.broadcast_to(line, (padded, groups)), 0.0),
            axis=1, keepdims=True,
        )
        spot = iota((padded, 1), 0)
        own = jnp.where(spot == padded - 1, jnp.broadcast_to(left[:, groups - 1 :], (padded, 1)), own)
        return jnp.where(spot == groups, jnp.broadcast_to(right[:, :1], (padded, 1)), own)

    blocks = vb_ref.shape[0]

    def flag_row(dr, k):
        rows = [
            vb_ref[k : k + 1, :] if (dr, dc) == (0, 0) else flags[place(dr, dc), k : k + 1, :]
            for dc in (-1, 0, 1)
        ]
        left, line, right = [row.astype(F32) for row in rows]
        return column(line, left, right)

    masks = [flag_row(-1, blocks - 1)] + [flag_row(0, k) for k in range(blocks)] + [flag_row(1, 0)]
    deblock_bias = jnp.concatenate([db_ref[...]] * 4, axis=1)
    per = half // blocks
    for k in range(half + 2):
        part = conv[k * padded : (k + 1) * padded]
        which = 0 if k == 0 else blocks + 1 if k == half + 1 else 1 + (k - 1) // per
        pooled[k] = (
            part[:, 4 * CH :] + masks[which] * (part[:, : 4 * CH] + deblock_bias)
        ).astype(BF16)

    def band_copy(to):
        return pltpu.make_async_remote_copy(
            src_ref=pooled.at[pl.ds(to * stride, stride + 2)],
            dst_ref=bands_in.at[me],
            send_sem=band_send.at[to],
            recv_sem=band_recv.at[me],
            device_id={"tm": to},
            device_id_type=MESH,
        )

    def band_arrival(source):
        return pltpu.make_async_remote_copy(
            src_ref=pooled.at[pl.ds(0, stride + 2)],
            dst_ref=bands_in.at[source],
            send_sem=band_send.at[source],
            recv_sem=band_recv.at[source],
            device_id={"tm": source},
            device_id_type=MESH,
        )

    first, last = jnp.int32(0), jnp.int32(n - 1)
    order = []
    for _ in range(n - 1):
        down = me - first > last - me
        to = jnp.where(down, first, last)
        band_copy(to).start()
        order.append(to)
        first, last = jnp.where(down, first + 1, first), jnp.where(down, last, last - 1)
    for load in loads[4:]:
        load.wait()
    encoder_matrix(ew_ref, tenc)
    slots = []
    for t in range(n):
        if n <= 8:
            slot = jnp.int32(0)
            for s in range(n):
                slot = jnp.where(owner_ref[s] == t, s, slot)
        else:
            slot = lax.fori_loop(
                0, n, lambda s, held: jnp.where(owner_ref[s] == t, s, held), jnp.int32(0)
            )
        slots.append(slot)

    def encode(frame, lines_in):
        shifted = []
        for own in lines_in:
            side = jnp.where(
                lanes_of >= 3 * CH,
                pltpu.roll(own, 1, 0),
                jnp.where(lanes_of < CH, pltpu.roll(own, padded - 1, 0), 0.0),
            )
            shifted.append(jnp.concatenate([own, side], axis=1))
        rows = [jnp.concatenate(shifted[k : k + 3], axis=1) for k in range(stride)]
        found = jnp.dot(
            jnp.concatenate(rows, axis=0).astype(BF16), tenc[...], preferred_element_type=F32
        )
        product[frame] = found.reshape(stride, padded, 12 * OUTC)

    encode(me, [pooled[me * stride + k].astype(F32) for k in range(stride + 2)])
    for source in reversed(order):
        band_arrival(source).wait_recv()
        encode(source, [bands_in[source, k].astype(F32) for k in range(stride + 2)])

    width = 4 * OUTC
    encoder_bias = jnp.concatenate([eb_ref[...]] * 4, axis=1)
    for t in range(1, n):
        for k in range(stride):
            total = encoder_bias
            for lag in range(3):
                total = total + product[slots[max(t - lag, 0)], k, :, lag * width : (lag + 1) * width]
            for j in range(2):
                lines[j, line_of((t - 1) * stride + k), :] = total[:, j * 4 * CH : (j + 1) * 4 * CH]
    for h in range(0, (n - 1) * stride, 8):
        count = min(8, (n - 1) * stride - h)
        for q in range(2 * groups):
            out_ref[h : h + count, q * 4 * CH : (q + 1) * 4 * CH] = lines[
                q % 2, pl.ds(h * padded + q // 2, count, stride=padded), :
            ].astype(BF16)

    for dr, dc in DIRECTIONS:

        @pl.when(exists(dr, dc))
        def _():
            for copy in copies(dr, dc):
                copy.wait_send()

    for d in range(1, n):
        band_copy(lax.rem(me + d, n)).wait_send()


def on_device(
    sizes, frames, owner_map, valid_blocks, deblock_weight, deblock_bias, encoder_weight, encoder_bias
):
    n = sizes[0]
    _, height, lanes = frames.shape
    raw = frames[0]
    groups = lanes // (8 * CH)
    padded = -(-(groups + 2) // 8) * 8
    blocks = valid_blocks.shape[1]
    half = height // 2
    stride = half // n
    vmem = pl.BlockSpec(memory_space=pltpu.VMEM)
    operands = (
        owner_map, raw, valid_blocks[0], deblock_weight.T, deblock_bias[None], encoder_weight.T,
        encoder_bias[None],
    )
    encoded = pl.pallas_call(
        functools.partial(kernel, sizes),
        out_shape=jax.ShapeDtypeStruct(((n - 1) * stride, groups * 4 * OUTC), BF16),
        in_specs=[pl.BlockSpec(memory_space=pltpu.HBM)] * 7,
        out_specs=vmem,
        scratch_shapes=[
            pltpu.SMEM((n,), jnp.int32),
            pltpu.VMEM((height, lanes), BF16),
            pltpu.VMEM((blocks, groups), jnp.int32),
            pltpu.VMEM((CH, 9 * CH), BF16),
            pltpu.VMEM((1, CH), F32),
            pltpu.VMEM((OUTC, 27 * CH), BF16),
            pltpu.VMEM((1, OUTC), F32),
            pltpu.VMEM((3, (height + 6) * padded, 4 * CH), F32),
            pltpu.VMEM((2, 3, padded, 8 * CH), BF16),
            pltpu.VMEM((2, 3, padded, 8 * CH), BF16),
            pltpu.VMEM((9, height, 4 * CH), BF16),
            pltpu.VMEM((9, blocks, groups), jnp.int32),
            pltpu.VMEM((48 * CH, 8 * CH), BF16),
            pltpu.VMEM((24 * CH, 12 * OUTC), BF16),
            pltpu.VMEM((half + 2, padded, 4 * CH), BF16),
            pltpu.VMEM((n, stride + 2, padded, 4 * CH), BF16),
            pltpu.VMEM((n, stride, padded, 12 * OUTC), F32),
            pltpu.VMEM((2, (n - 1) * stride * padded, 4 * CH), F32),
            pltpu.SemaphoreType.DMA((7,)),
            pltpu.SemaphoreType.DMA((9, 2)),
            pltpu.SemaphoreType.DMA((9, 2)),
            pltpu.SemaphoreType.DMA((n,)),
            pltpu.SemaphoreType.DMA((n,)),
        ],
        compiler_params=pltpu.CompilerParams(
            collective_id=0, has_side_effects=True, vmem_limit_bytes=40 * 1024 * 1024
        ),
    )(*[pltpu.with_memory_space_constraint(operand, pltpu.HBM) for operand in operands])
    return encoded.reshape(n - 1, 1, stride, groups * 4 * OUTC)


def solution(mesh):
    sizes = (mesh.shape["tm"], mesh.shape["row"], mesh.shape["col"])
    return jax.shard_map(
        functools.partial(on_device, sizes),
        mesh=mesh,
        in_specs=(
            P(("grp", "tm"), "row", "col"),
            P("grp"),
            P(("grp", "tm"), "row", "col"),
            P(),
            P(),
            P(),
            P(),
        ),
        out_specs=P("grp", "row", "tm", "col"),
        check_vma=False,
    )
```

```python
import functools

import jax
import jax.numpy as jnp
from jax import lax
from jax.experimental import pallas as pl
from jax.experimental.pallas import tpu as pltpu
from jax.sharding import PartitionSpec as P

CH = 32
OUTC = 64
MESH = pl.DeviceIdType.MESH
F32 = jnp.float32
BF16 = jnp.bfloat16


def place(dr, dc):
    return (dr + 1) * 3 + dc + 1


DIRECTIONS = [(dr, dc) for dr in (-1, 0, 1) for dc in (-1, 0, 1) if (dr, dc) != (0, 0)]


def iota(shape, dim):
    return lax.broadcasted_iota(jnp.int32, shape, dim)


def spread_taps(taps, spread):
    return lax.dot_general(taps, spread, (((0,), (0,)), ((), ())), preferred_element_type=F32)


def deblock_matrix(dw_ref, t_ref):
    block = iota((CH, 4 * CH), 1) // CH
    same = iota((CH, 4 * CH), 1) - block * CH == iota((CH, 4 * CH), 0)
    spread = same.astype(BF16)
    tiled = spread_taps(dw_ref[...], spread)
    taps = [[tiled[(3 * a + b) * CH : (3 * a + b + 1) * CH] for b in range(3)] for a in range(3)]
    wide = [
        [sum(row[b] for b in (d - 1, d) if 0 <= b < 3) for d in range(4)]
        for row in taps
    ]
    four = [
        [0.25 * sum(wide[a][d] for a in (e - 1, e) if 0 <= a < 3) for d in range(4)]
        for e in range(4)
    ]
    zero = jnp.zeros((CH, 4 * CH), F32)
    quarter = jnp.where(same, 0.25, 0.0)
    means = [jnp.where(block == o, quarter, zero).astype(BF16) for o in range(4)]
    nothing = jnp.zeros((8 * CH, 4 * CH), BF16)
    for e in range(4):
        base = e * 12 * CH

        def put(at, pixel):
            total = zero
            for o in range(4):
                d = pixel - 2 * o + 1
                if 0 <= d < 4:
                    total = jnp.where(block == o, four[e][d], total)
            t_ref[base + at * CH : base + (at + 1) * CH, : 4 * CH] = total.astype(BF16)

        for pixel in range(8):
            put(pixel, pixel)
        put(8, 8)
        put(11, -1)
        t_ref[base + 9 * CH : base + 11 * CH, : 4 * CH] = nothing[: 2 * CH]
        for pixel in range(8):
            t_ref[base + pixel * CH : base + (pixel + 1) * CH, 4 * CH :] = (
                means[pixel // 2] if e in (1, 2) else nothing[:CH]
            )
        t_ref[base + 8 * CH : base + 12 * CH, 4 * CH :] = nothing[: 4 * CH]


def encoder_matrix(ew_ref, t_ref):
    pair = 2 * OUTC
    rows, cols = iota((OUTC, 2 * pair), 0), iota((OUTC, 2 * pair), 1)
    spread = ((cols == rows) | (cols == rows + pair + OUTC)).astype(BF16)
    everything = spread_taps(ew_ref[...], spread).astype(BF16)
    nothing = jnp.zeros((2 * CH, 2 * pair), BF16)
    for lag in range(3):
        for dy in range(3):
            base = dy * 8 * CH
            left = lag * 2 * pair
            first = (lag * 9 + dy * 3) * CH

            def put(at, pixel):
                for side in range(2):
                    total = None
                    for o in (2 * side, 2 * side + 1):
                        d = pixel - o + 1
                        if 0 <= d < 3:
                            tap = everything[
                                first + d * CH : first + (d + 1) * CH, (o % 2) * pair : (o % 2 + 1) * pair
                            ]
                            total = tap if total is None else total + tap
                    if total is None:
                        total = nothing[:CH, :pair]
                    t_ref[
                        base + at * CH : base + (at + 1) * CH, left + side * pair : left + (side + 1) * pair
                    ] = total

            for pixel in range(4):
                put(pixel, pixel)
            put(4, 4)
            put(7, -1)
            t_ref[base + 5 * CH : base + 7 * CH, left : left + 2 * pair] = nothing


def kernel(
    sizes,
    owner_hbm,
    raw_hbm,
    vb_hbm,
    dw_hbm,
    db_hbm,
    ew_hbm,
    eb_hbm,
    out_ref,
    owner_ref,
    raw_ref,
    vb_ref,
    dw_ref,
    db_ref,
    ew_ref,
    eb_ref,
    ext,
    outgoing,
    halo,
    edge,
    flags,
    tdeb,
    tenc,
    pooled,
    bands_in,
    product,
    lines,
    load_sem,
    send_sem,
    recv_sem,
    band_send,
    band_recv,
):
    n, nr, nc = sizes
    height, width = raw_ref.shape
    groups = width // (8 * CH)
    padded = halo.shape[2]
    half = height // 2
    stride = half // n
    me = lax.axis_index("tm")
    r = lax.axis_index("row")
    c = lax.axis_index("col")

    loads = [
        pltpu.make_async_copy(a, b, load_sem.at[k])
        for k, (a, b) in enumerate(
            (
                (raw_hbm, raw_ref),
                (vb_hbm, vb_ref),
                (dw_hbm, dw_ref),
                (db_hbm, db_ref),
                (ew_hbm, ew_ref),
                (eb_hbm, eb_ref),
                (owner_hbm, owner_ref),
            )
        )
    ]
    for load in loads:
        load.start()

    halo[...] = jnp.zeros_like(halo)
    edge[...] = jnp.zeros_like(edge)
    flags[...] = jnp.zeros_like(flags)

    def exists(dr, dc):
        found = None
        for step, at, count in ((dr, r, nr), (dc, c, nc)):
            if step:
                inside = at > 0 if step < 0 else at < count - 1
                found = inside if found is None else jnp.logical_and(found, inside)
        return found

    def copies(dr, dc):
        here, there = place(dr, dc), place(-dr, -dc)
        to = {}
        if dr:
            to["row"] = r + dr
        if dc:
            to["col"] = c + dc
        if dc:
            lanes = pl.ds(0, 4 * CH) if dc < 0 else pl.ds(raw_ref.shape[1] - 4 * CH, 4 * CH)
            src, dst = raw_ref.at[:, lanes], edge.at[there]
        else:
            src = outgoing.at[0 if dr < 0 else 1]
            dst = halo.at[1 if dr < 0 else 0]
        return [
            pltpu.make_async_remote_copy(
                src_ref=a, dst_ref=b, send_sem=send_sem.at[here, k], recv_sem=recv_sem.at[there, k],
                device_id=to, device_id_type=MESH,
            )
            for k, (a, b) in enumerate(((src, dst), (vb_ref, flags.at[there])))
        ]

    barrier = pltpu.get_barrier_semaphore()
    for dr, dc in DIRECTIONS:
        to = {}
        if dr:
            to["row"] = r + dr
        if dc:
            to["col"] = c + dc

        @pl.when(exists(dr, dc))
        def _():
            pl.semaphore_signal(barrier, inc=1, device_id=to, device_id_type=MESH)

    for d in range(1, n):
        pl.semaphore_signal(
            barrier, inc=1, device_id={"tm": lax.rem(me + d, n)}, device_id_type=MESH
        )
    ext[...] = jnp.zeros_like(ext)

    def line_of(k):
        return pl.ds(k * padded, padded)

    loads[0].wait()
    for h in range(0, height, 8):
        for q in range(2 * groups):
            ext[q % 2, pl.ds((3 + h) * padded + q // 2, 8, stride=padded), :] = raw_ref[
                h : h + 8, q * 4 * CH : (q + 1) * 4 * CH
            ].astype(F32)
    for side, dr in enumerate((-1, 1)):

        @pl.when(exists(dr, 0))
        def _():
            for k in range(3):
                line = line_of(3 + k if dr < 0 else height + k)
                for j in range(2):
                    outgoing[side, k, :, j * 4 * CH : (j + 1) * 4 * CH] = ext[j, line, :].astype(BF16)

    loads[1].wait()
    tall = (r > 0).astype(jnp.int32) + (r < nr - 1).astype(jnp.int32) + 1
    broad = (c > 0).astype(jnp.int32) + (c < nc - 1).astype(jnp.int32) + 1
    pl.semaphore_wait(barrier, tall * broad - 1 + n - 1)

    for dr, dc in DIRECTIONS:

        @pl.when(exists(dr, dc))
        def _():
            for copy in copies(dr, dc):
                copy.start()

    lanes_of = iota((padded, 4 * CH), 1)

    def beside(k):
        before = pltpu.roll(ext[1, line_of(k), :], 1, 0)
        after = pltpu.roll(ext[0, line_of(k), :], padded - 1, 0)
        ext[2, line_of(k), :] = jnp.where(
            lanes_of >= 3 * CH, before, jnp.where(lanes_of < CH, after, 0.0)
        )

    for k in range(3, 3 + height):
        beside(k)
    loads[2].wait()
    loads[3].wait()
    deblock_matrix(dw_ref, tdeb)
    for load in loads[4:]:
        load.wait()
    encoder_matrix(ew_ref, tenc)

    for dr, dc in DIRECTIONS:

        @pl.when(exists(dr, dc))
        def _():
            for copy in copies(-dr, -dc):
                copy.wait_recv()

    for side, first in ((0, 0), (1, 3 + height)):
        for k in range(3):
            for j in range(2):
                ext[j, line_of(first + k), :] = halo[
                    side, k, :, j * 4 * CH : (j + 1) * 4 * CH
                ].astype(F32)
    for dc, at, j in ((-1, padded - 1, 1), (1, groups, 0)):
        for h in range(0, height, 8):
            ext[j, pl.ds((3 + h) * padded + at, 8, stride=padded), :] = edge[
                place(0, dc), h : h + 8
            ].astype(F32)
        top = edge[place(-1, dc)].astype(F32)
        low = edge[place(1, dc)].astype(F32)
        for k in range(3):
            for line, first in ((top[height - 3 + k : height - 2 + k], k), (low[k : k + 1], 3 + height + k)):
                ext[j, first * padded + at : first * padded + at + 1, :] = line

    for k in (0, 1, 2, height + 3, height + 4, height + 5):
        beside(k)
    lane = iota((8, 4 * CH), 1)
    for h in range(0, height, 8):
        for side, at, j in ((0, 0, padded - 1), (1, groups - 1, groups)):
            spot = pl.ds((3 + h) * padded + at, 8, stride=padded)
            chosen = lane >= 3 * CH if side == 0 else lane < CH
            came = edge[place(0, -1 if side == 0 else 1), h : h + 8].astype(F32)
            ext[2, spot, :] = jnp.where(chosen, came, ext[2, spot, :])

    lhs = jnp.concatenate(
        [
            jnp.concatenate([ext[j, line_of(2 * k + e), :] for e in range(4) for j in range(3)], axis=1)
            for k in range(half + 2)
        ],
        axis=0,
    ).astype(BF16)
    conv = jnp.dot(lhs, tdeb[...], preferred_element_type=F32)

    def column(line, left, right):
        spot = iota((padded, groups), 0)
        own = jnp.sum(
            jnp.where(spot == iota((padded, groups), 1), jnp.broadcast_to(line, (padded, groups)), 0.0),
            axis=1, keepdims=True,
        )
        spot = iota((padded, 1), 0)
        own = jnp.where(spot == padded - 1, jnp.broadcast_to(left[:, groups - 1 :], (padded, 1)), own)
        return jnp.where(spot == groups, jnp.broadcast_to(right[:, :1], (padded, 1)), own)

    blocks = vb_ref.shape[0]

    def flag_row(dr, k):
        rows = [
            vb_ref[k : k + 1, :] if (dr, dc) == (0, 0) else flags[place(dr, dc), k : k + 1, :]
            for dc in (-1, 0, 1)
        ]
        left, line, right = [row.astype(F32) for row in rows]
        return column(line, left, right)

    masks = [flag_row(-1, blocks - 1)] + [flag_row(0, k) for k in range(blocks)] + [flag_row(1, 0)]
    deblock_bias = jnp.concatenate([db_ref[...]] * 4, axis=1)
    per = half // blocks
    for k in range(half + 2):
        part = conv[k * padded : (k + 1) * padded]
        which = 0 if k == 0 else blocks + 1 if k == half + 1 else 1 + (k - 1) // per
        pooled[k] = (
            part[:, 4 * CH :] + masks[which] * (part[:, : 4 * CH] + deblock_bias)
        ).astype(BF16)

    def band_copy(to):
        return pltpu.make_async_remote_copy(
            src_ref=pooled.at[pl.ds(to * stride, stride + 2)],
            dst_ref=bands_in.at[me],
            send_sem=band_send.at[to],
            recv_sem=band_recv.at[me],
            device_id={"tm": to},
            device_id_type=MESH,
        )

    def band_arrival(source):
        return pltpu.make_async_remote_copy(
            src_ref=pooled.at[pl.ds(0, stride + 2)],
            dst_ref=bands_in.at[source],
            send_sem=band_send.at[source],
            recv_sem=band_recv.at[source],
            device_id={"tm": source},
            device_id_type=MESH,
        )

    first, last = jnp.int32(0), jnp.int32(n - 1)
    order = []
    for _ in range(n - 1):
        down = me - first > last - me
        to = jnp.where(down, first, last)
        band_copy(to).start()
        order.append(to)
        first, last = jnp.where(down, first + 1, first), jnp.where(down, last, last - 1)
    slots = []
    for t in range(n):
        if n <= 8:
            slot = jnp.int32(0)
            for s in range(n):
                slot = jnp.where(owner_ref[s] == t, s, slot)
        else:
            slot = lax.fori_loop(
                0, n, lambda s, held: jnp.where(owner_ref[s] == t, s, held), jnp.int32(0)
            )
        slots.append(slot)

    def encode(frames, lines_in):
        rows = []
        for lines_of_frame in lines_in:
            shifted = []
            for own in lines_of_frame:
                side = jnp.where(
                    lanes_of >= 3 * CH,
                    pltpu.roll(own, 1, 0),
                    jnp.where(lanes_of < CH, pltpu.roll(own, padded - 1, 0), 0.0),
                )
                shifted.append(jnp.concatenate([own, side], axis=1))
            rows += [jnp.concatenate(shifted[k : k + 3], axis=1) for k in range(stride)]
        found = jnp.dot(
            jnp.concatenate(rows, axis=0).astype(BF16), tenc[...], preferred_element_type=F32
        ).reshape(len(frames), stride, padded, 12 * OUTC)
        for k, frame in enumerate(frames):
            product[frame] = found[k]

    encode([me], [[pooled[me * stride + k].astype(F32) for k in range(stride + 2)]])
    for source in order:
        band_arrival(source).wait_recv()
    encode(order, [[bands_in[s, k].astype(F32) for k in range(stride + 2)] for s in order])

    width = 4 * OUTC
    encoder_bias = jnp.concatenate([eb_ref[...]] * 4, axis=1)
    for t in range(1, n):
        for k in range(stride):
            total = encoder_bias
            for lag in range(3):
                total = total + product[slots[max(t - lag, 0)], k, :, lag * width : (lag + 1) * width]
            for j in range(2):
                lines[j, line_of((t - 1) * stride + k), :] = total[:, j * 4 * CH : (j + 1) * 4 * CH]
    for h in range(0, (n - 1) * stride, 8):
        count = min(8, (n - 1) * stride - h)
        for q in range(2 * groups):
            out_ref[h : h + count, q * 4 * CH : (q + 1) * 4 * CH] = lines[
                q % 2, pl.ds(h * padded + q // 2, count, stride=padded), :
            ].astype(BF16)

    for dr, dc in DIRECTIONS:

        @pl.when(exists(dr, dc))
        def _():
            for copy in copies(dr, dc):
                copy.wait_send()

    for d in range(1, n):
        band_copy(lax.rem(me + d, n)).wait_send()


def on_device(
    sizes, frames, owner_map, valid_blocks, deblock_weight, deblock_bias, encoder_weight, encoder_bias
):
    n = sizes[0]
    _, height, lanes = frames.shape
    raw = frames[0]
    groups = lanes // (8 * CH)
    padded = -(-(groups + 2) // 8) * 8
    blocks = valid_blocks.shape[1]
    half = height // 2
    stride = half // n
    vmem = pl.BlockSpec(memory_space=pltpu.VMEM)
    operands = (
        owner_map, raw, valid_blocks[0], deblock_weight.T, deblock_bias[None], encoder_weight.T,
        encoder_bias[None],
    )
    encoded = pl.pallas_call(
        functools.partial(kernel, sizes),
        out_shape=jax.ShapeDtypeStruct(((n - 1) * stride, groups * 4 * OUTC), BF16),
        in_specs=[pl.BlockSpec(memory_space=pltpu.HBM)] * 7,
        out_specs=vmem,
        scratch_shapes=[
            pltpu.SMEM((n,), jnp.int32),
            pltpu.VMEM((height, lanes), BF16),
            pltpu.VMEM((blocks, groups), jnp.int32),
            pltpu.VMEM((CH, 9 * CH), BF16),
            pltpu.VMEM((1, CH), F32),
            pltpu.VMEM((OUTC, 27 * CH), BF16),
            pltpu.VMEM((1, OUTC), F32),
            pltpu.VMEM((3, (height + 6) * padded, 4 * CH), F32),
            pltpu.VMEM((2, 3, padded, 8 * CH), BF16),
            pltpu.VMEM((2, 3, padded, 8 * CH), BF16),
            pltpu.VMEM((9, height, 4 * CH), BF16),
            pltpu.VMEM((9, blocks, groups), jnp.int32),
            pltpu.VMEM((48 * CH, 8 * CH), BF16),
            pltpu.VMEM((24 * CH, 12 * OUTC), BF16),
            pltpu.VMEM((half + 2, padded, 4 * CH), BF16),
            pltpu.VMEM((n, stride + 2, padded, 4 * CH), BF16),
            pltpu.VMEM((n, stride, padded, 12 * OUTC), F32),
            pltpu.VMEM((2, (n - 1) * stride * padded, 4 * CH), F32),
            pltpu.SemaphoreType.DMA((7,)),
            pltpu.SemaphoreType.DMA((9, 2)),
            pltpu.SemaphoreType.DMA((9, 2)),
            pltpu.SemaphoreType.DMA((n,)),
            pltpu.SemaphoreType.DMA((n,)),
        ],
        compiler_params=pltpu.CompilerParams(
            collective_id=0, has_side_effects=True, vmem_limit_bytes=40 * 1024 * 1024
        ),
    )(*[pltpu.with_memory_space_constraint(operand, pltpu.HBM) for operand in operands])
    return encoded.reshape(n - 1, 1, stride, groups * 4 * OUTC)


def solution(mesh):
    sizes = (mesh.shape["tm"], mesh.shape["row"], mesh.shape["col"])
    return jax.shard_map(
        functools.partial(on_device, sizes),
        mesh=mesh,
        in_specs=(
            P(("grp", "tm"), "row", "col"),
            P("grp"),
            P(("grp", "tm"), "row", "col"),
            P(),
            P(),
            P(),
            P(),
        ),
        out_specs=P("grp", "row", "tm", "col"),
        check_vma=False,
    )
```

```python
import functools

import jax
import jax.numpy as jnp
from jax import lax
from jax.experimental import pallas as pl
from jax.experimental.pallas import tpu as pltpu
from jax.sharding import PartitionSpec as P

CH = 32
OUTC = 64
MESH = pl.DeviceIdType.MESH
F32 = jnp.float32
BF16 = jnp.bfloat16


def place(dr, dc):
    return (dr + 1) * 3 + dc + 1


DIRECTIONS = [(dr, dc) for dr in (-1, 0, 1) for dc in (-1, 0, 1) if (dr, dc) != (0, 0)]


def iota(shape, dim):
    return lax.broadcasted_iota(jnp.int32, shape, dim)


def spread_taps(taps, spread):
    return lax.dot_general(taps, spread, (((0,), (0,)), ((), ())), preferred_element_type=F32)


def deblock_matrix(dw_ref, t_ref):
    block = iota((CH, 4 * CH), 1) // CH
    same = iota((CH, 4 * CH), 1) - block * CH == iota((CH, 4 * CH), 0)
    spread = same.astype(BF16)
    tiled = spread_taps(dw_ref[...], spread)
    taps = [[tiled[(3 * a + b) * CH : (3 * a + b + 1) * CH] for b in range(3)] for a in range(3)]
    wide = [
        [sum(row[b] for b in (d - 1, d) if 0 <= b < 3) for d in range(4)]
        for row in taps
    ]
    four = [
        [0.25 * sum(wide[a][d] for a in (e - 1, e) if 0 <= a < 3) for d in range(4)]
        for e in range(4)
    ]
    zero = jnp.zeros((CH, 4 * CH), F32)
    quarter = jnp.where(same, 0.25, 0.0)
    means = [jnp.where(block == o, quarter, zero).astype(BF16) for o in range(4)]
    nothing = jnp.zeros((8 * CH, 4 * CH), BF16)
    for e in range(4):
        base = e * 12 * CH

        def put(at, pixel):
            total = zero
            for o in range(4):
                d = pixel - 2 * o + 1
                if 0 <= d < 4:
                    total = jnp.where(block == o, four[e][d], total)
            t_ref[base + at * CH : base + (at + 1) * CH, : 4 * CH] = total.astype(BF16)

        for pixel in range(8):
            put(pixel, pixel)
        put(8, 8)
        put(11, -1)
        t_ref[base + 9 * CH : base + 11 * CH, : 4 * CH] = nothing[: 2 * CH]
        for pixel in range(8):
            t_ref[base + pixel * CH : base + (pixel + 1) * CH, 4 * CH :] = (
                means[pixel // 2] if e in (1, 2) else nothing[:CH]
            )
        t_ref[base + 8 * CH : base + 12 * CH, 4 * CH :] = nothing[: 4 * CH]


def encoder_matrix(ew_ref, t_ref):
    pair = 2 * OUTC
    rows, cols = iota((OUTC, 2 * pair), 0), iota((OUTC, 2 * pair), 1)
    spread = ((cols == rows) | (cols == rows + pair + OUTC)).astype(BF16)
    everything = spread_taps(ew_ref[...], spread).astype(BF16)
    nothing = jnp.zeros((2 * CH, 2 * pair), BF16)
    for lag in range(3):
        for dy in range(3):
            base = dy * 8 * CH
            left = lag * 2 * pair
            first = (lag * 9 + dy * 3) * CH

            def put(at, pixel):
                for side in range(2):
                    total = None
                    for o in (2 * side, 2 * side + 1):
                        d = pixel - o + 1
                        if 0 <= d < 3:
                            tap = everything[
                                first + d * CH : first + (d + 1) * CH, (o % 2) * pair : (o % 2 + 1) * pair
                            ]
                            total = tap if total is None else total + tap
                    if total is None:
                        total = nothing[:CH, :pair]
                    t_ref[
                        base + at * CH : base + (at + 1) * CH, left + side * pair : left + (side + 1) * pair
                    ] = total

            for pixel in range(4):
                put(pixel, pixel)
            put(4, 4)
            put(7, -1)
            t_ref[base + 5 * CH : base + 7 * CH, left : left + 2 * pair] = nothing


def kernel(
    sizes,
    owner_hbm,
    raw_hbm,
    vb_hbm,
    dw_hbm,
    db_hbm,
    ew_hbm,
    eb_hbm,
    out_ref,
    owner_ref,
    raw_ref,
    vb_ref,
    dw_ref,
    db_ref,
    ew_ref,
    eb_ref,
    ext,
    outgoing,
    halo,
    edge,
    flags,
    tdeb,
    tenc,
    pooled,
    bands_in,
    product,
    lines,
    load_sem,
    send_sem,
    recv_sem,
    band_send,
    band_recv,
):
    n, nr, nc = sizes
    height, width = raw_ref.shape
    groups = width // (8 * CH)
    padded = halo.shape[2]
    half = height // 2
    stride = half // n
    me = lax.axis_index("tm")
    r = lax.axis_index("row")
    c = lax.axis_index("col")

    loads = [
        pltpu.make_async_copy(a, b, load_sem.at[k])
        for k, (a, b) in enumerate(
            (
                (raw_hbm, raw_ref),
                (vb_hbm, vb_ref),
                (dw_hbm, dw_ref),
                (db_hbm, db_ref),
                (ew_hbm, ew_ref),
                (eb_hbm, eb_ref),
                (owner_hbm, owner_ref),
            )
        )
    ]
    for load in loads:
        load.start()

    halo[...] = jnp.zeros_like(halo)
    edge[...] = jnp.zeros_like(edge)
    flags[...] = jnp.zeros_like(flags)

    def exists(dr, dc):
        found = None
        for step, at, count in ((dr, r, nr), (dc, c, nc)):
            if step:
                inside = at > 0 if step < 0 else at < count - 1
                found = inside if found is None else jnp.logical_and(found, inside)
        return found

    def copies(dr, dc):
        here, there = place(dr, dc), place(-dr, -dc)
        to = {}
        if dr:
            to["row"] = r + dr
        if dc:
            to["col"] = c + dc
        if dc:
            lanes = pl.ds(0, 4 * CH) if dc < 0 else pl.ds(raw_ref.shape[1] - 4 * CH, 4 * CH)
            src, dst = raw_ref.at[:, lanes], edge.at[there]
        else:
            src = outgoing.at[0 if dr < 0 else 1]
            dst = halo.at[1 if dr < 0 else 0]
        return [
            pltpu.make_async_remote_copy(
                src_ref=a, dst_ref=b, send_sem=send_sem.at[here, k], recv_sem=recv_sem.at[there, k],
                device_id=to, device_id_type=MESH,
            )
            for k, (a, b) in enumerate(((src, dst), (vb_ref, flags.at[there])))
        ]

    barrier = pltpu.get_barrier_semaphore()
    for dr, dc in DIRECTIONS:
        to = {}
        if dr:
            to["row"] = r + dr
        if dc:
            to["col"] = c + dc

        @pl.when(exists(dr, dc))
        def _():
            pl.semaphore_signal(barrier, inc=1, device_id=to, device_id_type=MESH)

    for d in range(1, n):
        pl.semaphore_signal(
            barrier, inc=1, device_id={"tm": lax.rem(me + d, n)}, device_id_type=MESH
        )
    ext[...] = jnp.zeros_like(ext)

    def line_of(k):
        return pl.ds(k * padded, padded)

    loads[0].wait()
    for h in range(0, height, 8):
        for q in range(2 * groups):
            ext[q % 2, pl.ds((3 + h) * padded + q // 2, 8, stride=padded), :] = raw_ref[
                h : h + 8, q * 4 * CH : (q + 1) * 4 * CH
            ].astype(F32)
    for side, dr in enumerate((-1, 1)):

        @pl.when(exists(dr, 0))
        def _():
            for k in range(3):
                line = line_of(3 + k if dr < 0 else height + k)
                for j in range(2):
                    outgoing[side, k, :, j * 4 * CH : (j + 1) * 4 * CH] = ext[j, line, :].astype(BF16)

    for load in loads[1:]:
        load.wait()

    @pl.when(me < n // 2)
    def _():
        encoder_matrix(ew_ref, tenc)

    tall = (r > 0).astype(jnp.int32) + (r < nr - 1).astype(jnp.int32) + 1
    broad = (c > 0).astype(jnp.int32) + (c < nc - 1).astype(jnp.int32) + 1
    pl.semaphore_wait(barrier, tall * broad - 1 + n - 1)

    for dr, dc in DIRECTIONS:

        @pl.when(exists(dr, dc))
        def _():
            for copy in copies(dr, dc):
                copy.start()

    lanes_of = iota((padded, 4 * CH), 1)

    def beside(k):
        before = pltpu.roll(ext[1, line_of(k), :], 1, 0)
        after = pltpu.roll(ext[0, line_of(k), :], padded - 1, 0)
        ext[2, line_of(k), :] = jnp.where(
            lanes_of >= 3 * CH, before, jnp.where(lanes_of < CH, after, 0.0)
        )

    for k in range(3, 3 + height):
        beside(k)
    deblock_matrix(dw_ref, tdeb)

    for dr, dc in DIRECTIONS:

        @pl.when(exists(dr, dc))
        def _():
            for copy in copies(-dr, -dc):
                copy.wait_recv()

    for side, first in ((0, 0), (1, 3 + height)):
        for k in range(3):
            for j in range(2):
                ext[j, line_of(first + k), :] = halo[
                    side, k, :, j * 4 * CH : (j + 1) * 4 * CH
                ].astype(F32)
    for dc, at, j in ((-1, padded - 1, 1), (1, groups, 0)):
        for h in range(0, height, 8):
            ext[j, pl.ds((3 + h) * padded + at, 8, stride=padded), :] = edge[
                place(0, dc), h : h + 8
            ].astype(F32)
        top = edge[place(-1, dc)].astype(F32)
        low = edge[place(1, dc)].astype(F32)
        for k in range(3):
            for line, first in ((top[height - 3 + k : height - 2 + k], k), (low[k : k + 1], 3 + height + k)):
                ext[j, first * padded + at : first * padded + at + 1, :] = line

    for k in (0, 1, 2, height + 3, height + 4, height + 5):
        beside(k)
    lane = iota((8, 4 * CH), 1)
    for h in range(0, height, 8):
        for side, at, j in ((0, 0, padded - 1), (1, groups - 1, groups)):
            spot = pl.ds((3 + h) * padded + at, 8, stride=padded)
            chosen = lane >= 3 * CH if side == 0 else lane < CH
            came = edge[place(0, -1 if side == 0 else 1), h : h + 8].astype(F32)
            ext[2, spot, :] = jnp.where(chosen, came, ext[2, spot, :])

    lhs = jnp.concatenate(
        [
            jnp.concatenate([ext[j, line_of(2 * k + e), :] for e in range(4) for j in range(3)], axis=1)
            for k in range(half + 2)
        ],
        axis=0,
    ).astype(BF16)
    conv = jnp.dot(lhs, tdeb[...], preferred_element_type=F32)

    def column(line, left, right):
        spot = iota((padded, groups), 0)
        own = jnp.sum(
            jnp.where(spot == iota((padded, groups), 1), jnp.broadcast_to(line, (padded, groups)), 0.0),
            axis=1, keepdims=True,
        )
        spot = iota((padded, 1), 0)
        own = jnp.where(spot == padded - 1, jnp.broadcast_to(left[:, groups - 1 :], (padded, 1)), own)
        return jnp.where(spot == groups, jnp.broadcast_to(right[:, :1], (padded, 1)), own)

    blocks = vb_ref.shape[0]

    def flag_row(dr, k):
        rows = [
            vb_ref[k : k + 1, :] if (dr, dc) == (0, 0) else flags[place(dr, dc), k : k + 1, :]
            for dc in (-1, 0, 1)
        ]
        left, line, right = [row.astype(F32) for row in rows]
        return column(line, left, right)

    masks = [flag_row(-1, blocks - 1)] + [flag_row(0, k) for k in range(blocks)] + [flag_row(1, 0)]
    deblock_bias = jnp.concatenate([db_ref[...]] * 4, axis=1)
    per = half // blocks
    for k in range(half + 2):
        part = conv[k * padded : (k + 1) * padded]
        which = 0 if k == 0 else blocks + 1 if k == half + 1 else 1 + (k - 1) // per
        pooled[k] = (
            part[:, 4 * CH :] + masks[which] * (part[:, : 4 * CH] + deblock_bias)
        ).astype(BF16)

    def band_copy(to):
        return pltpu.make_async_remote_copy(
            src_ref=pooled.at[pl.ds(to * stride, stride + 2)],
            dst_ref=bands_in.at[me],
            send_sem=band_send.at[to],
            recv_sem=band_recv.at[me],
            device_id={"tm": to},
            device_id_type=MESH,
        )

    def band_arrival(source):
        return pltpu.make_async_remote_copy(
            src_ref=pooled.at[pl.ds(0, stride + 2)],
            dst_ref=bands_in.at[source],
            send_sem=band_send.at[source],
            recv_sem=band_recv.at[source],
            device_id={"tm": source},
            device_id_type=MESH,
        )

    order = [jnp.where(me > k, k, k + 1) for k in range(n - 1)]
    for to in order:
        band_copy(to).start()

    @pl.when(me >= n // 2)
    def _():
        encoder_matrix(ew_ref, tenc)

    slots = []
    for t in range(n):
        if n <= 8:
            slot = jnp.int32(0)
            for s in range(n):
                slot = jnp.where(owner_ref[s] == t, s, slot)
        else:
            slot = lax.fori_loop(
                0, n, lambda s, held: jnp.where(owner_ref[s] == t, s, held), jnp.int32(0)
            )
        slots.append(slot)

    def encode(frames, lines_in):
        rows = []
        for lines_of_frame in lines_in:
            shifted = []
            for own in lines_of_frame:
                side = jnp.where(
                    lanes_of >= 3 * CH,
                    pltpu.roll(own, 1, 0),
                    jnp.where(lanes_of < CH, pltpu.roll(own, padded - 1, 0), 0.0),
                )
                shifted.append(jnp.concatenate([own, side], axis=1))
            rows += [jnp.concatenate(shifted[k : k + 3], axis=1) for k in range(stride)]
        found = jnp.dot(
            jnp.concatenate(rows, axis=0).astype(BF16), tenc[...], preferred_element_type=F32
        ).reshape(len(frames), stride, padded, 12 * OUTC)
        for k, frame in enumerate(frames):
            product[frame] = found[k]

    encode([me], [[pooled[me * stride + k].astype(F32) for k in range(stride + 2)]])
    for source in order:
        band_arrival(source).wait_recv()
    encode(order, [[bands_in[s, k].astype(F32) for k in range(stride + 2)] for s in order])

    width = 4 * OUTC
    encoder_bias = jnp.concatenate([eb_ref[...]] * 4, axis=1)
    for t in range(1, n):
        for k in range(stride):
            total = encoder_bias
            for lag in range(3):
                total = total + product[slots[max(t - lag, 0)], k, :, lag * width : (lag + 1) * width]
            for j in range(2):
                lines[j, line_of((t - 1) * stride + k), :] = total[:, j * 4 * CH : (j + 1) * 4 * CH]
    for h in range(0, (n - 1) * stride, 8):
        count = min(8, (n - 1) * stride - h)
        for q in range(2 * groups):
            out_ref[h : h + count, q * 4 * CH : (q + 1) * 4 * CH] = lines[
                q % 2, pl.ds(h * padded + q // 2, count, stride=padded), :
            ].astype(BF16)

    for dr, dc in DIRECTIONS:

        @pl.when(exists(dr, dc))
        def _():
            for copy in copies(dr, dc):
                copy.wait_send()

    for d in range(1, n):
        band_copy(lax.rem(me + d, n)).wait_send()


def on_device(
    sizes, frames, owner_map, valid_blocks, deblock_weight, deblock_bias, encoder_weight, encoder_bias
):
    n = sizes[0]
    _, height, lanes = frames.shape
    raw = frames[0]
    groups = lanes // (8 * CH)
    padded = -(-(groups + 2) // 8) * 8
    blocks = valid_blocks.shape[1]
    half = height // 2
    stride = half // n
    vmem = pl.BlockSpec(memory_space=pltpu.VMEM)
    operands = (
        owner_map, raw, valid_blocks[0], deblock_weight.T, deblock_bias[None], encoder_weight.T,
        encoder_bias[None],
    )
    encoded = pl.pallas_call(
        functools.partial(kernel, sizes),
        out_shape=jax.ShapeDtypeStruct(((n - 1) * stride, groups * 4 * OUTC), BF16),
        in_specs=[pl.BlockSpec(memory_space=pltpu.HBM)] * 7,
        out_specs=vmem,
        scratch_shapes=[
            pltpu.SMEM((n,), jnp.int32),
            pltpu.VMEM((height, lanes), BF16),
            pltpu.VMEM((blocks, groups), jnp.int32),
            pltpu.VMEM((CH, 9 * CH), BF16),
            pltpu.VMEM((1, CH), F32),
            pltpu.VMEM((OUTC, 27 * CH), BF16),
            pltpu.VMEM((1, OUTC), F32),
            pltpu.VMEM((3, (height + 6) * padded, 4 * CH), F32),
            pltpu.VMEM((2, 3, padded, 8 * CH), BF16),
            pltpu.VMEM((2, 3, padded, 8 * CH), BF16),
            pltpu.VMEM((9, height, 4 * CH), BF16),
            pltpu.VMEM((9, blocks, groups), jnp.int32),
            pltpu.VMEM((48 * CH, 8 * CH), BF16),
            pltpu.VMEM((24 * CH, 12 * OUTC), BF16),
            pltpu.VMEM((half + 2, padded, 4 * CH), BF16),
            pltpu.VMEM((n, stride + 2, padded, 4 * CH), BF16),
            pltpu.VMEM((n, stride, padded, 12 * OUTC), F32),
            pltpu.VMEM((2, (n - 1) * stride * padded, 4 * CH), F32),
            pltpu.SemaphoreType.DMA((7,)),
            pltpu.SemaphoreType.DMA((9, 2)),
            pltpu.SemaphoreType.DMA((9, 2)),
            pltpu.SemaphoreType.DMA((n,)),
            pltpu.SemaphoreType.DMA((n,)),
        ],
        compiler_params=pltpu.CompilerParams(
            collective_id=0, has_side_effects=True, vmem_limit_bytes=40 * 1024 * 1024
        ),
    )(*[pltpu.with_memory_space_constraint(operand, pltpu.HBM) for operand in operands])
    return encoded.reshape(n - 1, 1, stride, groups * 4 * OUTC)


def solution(mesh):
    sizes = (mesh.shape["tm"], mesh.shape["row"], mesh.shape["col"])
    return jax.shard_map(
        functools.partial(on_device, sizes),
        mesh=mesh,
        in_specs=(
            P(("grp", "tm"), "row", "col"),
            P("grp"),
            P(("grp", "tm"), "row", "col"),
            P(),
            P(),
            P(),
            P(),
        ),
        out_specs=P("grp", "row", "tm", "col"),
        check_vma=False,
    )
```

```python
import functools

import jax
import jax.numpy as jnp
from jax import lax
from jax.experimental import pallas as pl
from jax.experimental.pallas import tpu as pltpu
from jax.sharding import PartitionSpec as P

CH = 32
OUTC = 64
MESH = pl.DeviceIdType.MESH
F32 = jnp.float32
BF16 = jnp.bfloat16


def place(dr, dc):
    return (dr + 1) * 3 + dc + 1


DIRECTIONS = [(dr, dc) for dr in (-1, 0, 1) for dc in (-1, 0, 1) if (dr, dc) != (0, 0)]


def iota(shape, dim):
    return lax.broadcasted_iota(jnp.int32, shape, dim)


def spread_taps(taps, spread):
    return lax.dot_general(taps, spread, (((0,), (0,)), ((), ())), preferred_element_type=F32)


def deblock_matrix(dw_ref, t_ref):
    block = iota((CH, 4 * CH), 1) // CH
    same = iota((CH, 4 * CH), 1) - block * CH == iota((CH, 4 * CH), 0)
    spread = same.astype(BF16)
    tiled = spread_taps(dw_ref[...], spread)
    taps = [[tiled[(3 * a + b) * CH : (3 * a + b + 1) * CH] for b in range(3)] for a in range(3)]
    wide = [
        [sum(row[b] for b in (d - 1, d) if 0 <= b < 3) for d in range(4)]
        for row in taps
    ]
    four = [
        [0.25 * sum(wide[a][d] for a in (e - 1, e) if 0 <= a < 3) for d in range(4)]
        for e in range(4)
    ]
    zero = jnp.zeros((CH, 4 * CH), F32)
    quarter = jnp.where(same, 0.25, 0.0)
    means = [jnp.where(block == o, quarter, zero).astype(BF16) for o in range(4)]
    nothing = jnp.zeros((8 * CH, 4 * CH), BF16)
    for e in range(4):
        base = e * 12 * CH

        def put(at, pixel):
            total = zero
            for o in range(4):
                d = pixel - 2 * o + 1
                if 0 <= d < 4:
                    total = jnp.where(block == o, four[e][d], total)
            t_ref[base + at * CH : base + (at + 1) * CH, : 4 * CH] = total.astype(BF16)

        for pixel in range(8):
            put(pixel, pixel)
        put(8, 8)
        put(11, -1)
        t_ref[base + 9 * CH : base + 11 * CH, : 4 * CH] = nothing[: 2 * CH]
        for pixel in range(8):
            t_ref[base + pixel * CH : base + (pixel + 1) * CH, 4 * CH :] = (
                means[pixel // 2] if e in (1, 2) else nothing[:CH]
            )
        t_ref[base + 8 * CH : base + 12 * CH, 4 * CH :] = nothing[: 4 * CH]


def encoder_matrix(ew_ref, t_ref):
    pair = 2 * OUTC
    rows, cols = iota((OUTC, 2 * pair), 0), iota((OUTC, 2 * pair), 1)
    spread = ((cols == rows) | (cols == rows + pair + OUTC)).astype(BF16)
    everything = spread_taps(ew_ref[...], spread).astype(BF16)
    nothing = jnp.zeros((2 * CH, 2 * pair), BF16)
    for lag in range(3):
        for dy in range(3):
            base = dy * 8 * CH
            left = lag * 2 * pair
            first = (lag * 9 + dy * 3) * CH

            def put(at, pixel):
                for side in range(2):
                    total = None
                    for o in (2 * side, 2 * side + 1):
                        d = pixel - o + 1
                        if 0 <= d < 3:
                            tap = everything[
                                first + d * CH : first + (d + 1) * CH, (o % 2) * pair : (o % 2 + 1) * pair
                            ]
                            total = tap if total is None else total + tap
                    if total is None:
                        total = nothing[:CH, :pair]
                    t_ref[
                        base + at * CH : base + (at + 1) * CH, left + side * pair : left + (side + 1) * pair
                    ] = total

            for pixel in range(4):
                put(pixel, pixel)
            put(4, 4)
            put(7, -1)
            t_ref[base + 5 * CH : base + 7 * CH, left : left + 2 * pair] = nothing


def kernel(
    sizes,
    owner_hbm,
    raw_hbm,
    vb_hbm,
    dw_hbm,
    db_hbm,
    ew_hbm,
    eb_hbm,
    out_ref,
    owner_ref,
    raw_ref,
    vb_ref,
    dw_ref,
    db_ref,
    ew_ref,
    eb_ref,
    ext,
    outgoing,
    halo,
    edge,
    flags,
    tdeb,
    tenc,
    pooled,
    bands_in,
    product,
    lines,
    load_sem,
    send_sem,
    recv_sem,
    band_send,
    band_recv,
):
    n, nr, nc = sizes
    height, width = raw_ref.shape
    groups = width // (8 * CH)
    padded = pooled.shape[1]
    half = height // 2
    stride = half // n
    me = lax.axis_index("tm")
    r = lax.axis_index("row")
    c = lax.axis_index("col")

    loads = [
        pltpu.make_async_copy(a, b, load_sem.at[k])
        for k, (a, b) in enumerate(
            (
                (raw_hbm, raw_ref),
                (vb_hbm, vb_ref),
                (dw_hbm, dw_ref),
                (db_hbm, db_ref),
                (ew_hbm, ew_ref),
                (eb_hbm, eb_ref),
                (owner_hbm, owner_ref),
            )
        )
    ]
    for load in loads:
        load.start()

    halo[...] = jnp.zeros_like(halo)
    edge[...] = jnp.zeros_like(edge)
    flags[...] = jnp.zeros_like(flags)

    def exists(dr, dc):
        found = None
        for step, at, count in ((dr, r, nr), (dc, c, nc)):
            if step:
                inside = at > 0 if step < 0 else at < count - 1
                found = inside if found is None else jnp.logical_and(found, inside)
        return found

    def copies(dr, dc):
        here, there = place(dr, dc), place(-dr, -dc)
        to = {}
        if dr:
            to["row"] = r + dr
        if dc:
            to["col"] = c + dc
        if dc:
            lanes = pl.ds(0, 4 * CH) if dc < 0 else pl.ds(raw_ref.shape[1] - 4 * CH, 4 * CH)
            src, dst = raw_ref.at[:, lanes], edge.at[there]
        else:
            src = outgoing.at[0 if dr < 0 else 1]
            dst = halo.at[1 if dr < 0 else 0]
        return [
            pltpu.make_async_remote_copy(
                src_ref=a, dst_ref=b, send_sem=send_sem.at[here, k], recv_sem=recv_sem.at[there, k],
                device_id=to, device_id_type=MESH,
            )
            for k, (a, b) in enumerate(((src, dst), (vb_ref, flags.at[there])))
        ]

    barrier = pltpu.get_barrier_semaphore()
    for dr, dc in DIRECTIONS:
        to = {}
        if dr:
            to["row"] = r + dr
        if dc:
            to["col"] = c + dc

        @pl.when(exists(dr, dc))
        def _():
            pl.semaphore_signal(barrier, inc=1, device_id=to, device_id_type=MESH)

    for d in range(1, n):
        pl.semaphore_signal(
            barrier, inc=1, device_id={"tm": lax.rem(me + d, n)}, device_id_type=MESH
        )
    ext[...] = jnp.zeros_like(ext)

    def line_of(k):
        return pl.ds(k * padded, padded)

    loads[0].wait()
    for h in range(0, height, 8):
        for q in range(2 * groups):
            ext[q % 2, pl.ds((3 + h) * padded + q // 2, 8, stride=padded), :] = raw_ref[
                h : h + 8, q * 4 * CH : (q + 1) * 4 * CH
            ].astype(F32)
    for side, dr in enumerate((-1, 1)):

        @pl.when(exists(dr, 0))
        def _():
            for k in range(3):
                line = line_of(3 + k if dr < 0 else height + k)
                for j in range(2):
                    outgoing[side, k, :, j * 4 * CH : (j + 1) * 4 * CH] = ext[j, line, :][:groups].astype(BF16)

    for load in loads[1:]:
        load.wait()

    @pl.when(me < n // 2)
    def _():
        encoder_matrix(ew_ref, tenc)

    tall = (r > 0).astype(jnp.int32) + (r < nr - 1).astype(jnp.int32) + 1
    broad = (c > 0).astype(jnp.int32) + (c < nc - 1).astype(jnp.int32) + 1
    pl.semaphore_wait(barrier, tall * broad - 1 + n - 1)

    for k in range(2):
        for dr, dc in sorted(DIRECTIONS, key=lambda item: item[1] != 0):

            @pl.when(exists(dr, dc))
            def _():
                copies(dr, dc)[k].start()

    lanes_of = iota((padded, 4 * CH), 1)

    def beside(k):
        before = pltpu.roll(ext[1, line_of(k), :], 1, 0)
        after = pltpu.roll(ext[0, line_of(k), :], padded - 1, 0)
        ext[2, line_of(k), :] = jnp.where(
            lanes_of >= 3 * CH, before, jnp.where(lanes_of < CH, after, 0.0)
        )

    for k in range(3, 3 + height):
        beside(k)
    deblock_matrix(dw_ref, tdeb)

    for dr, dc in DIRECTIONS:

        @pl.when(exists(dr, dc))
        def _():
            for copy in copies(-dr, -dc):
                copy.wait_recv()

    for side, first in ((0, 0), (1, 3 + height)):
        for k in range(3):
            for j in range(2):
                ext[j, pl.ds((first + k) * padded, groups), :] = halo[
                    side, k, :, j * 4 * CH : (j + 1) * 4 * CH
                ].astype(F32)
    for dc, at, j in ((-1, padded - 1, 1), (1, groups, 0)):
        for h in range(0, height, 8):
            ext[j, pl.ds((3 + h) * padded + at, 8, stride=padded), :] = edge[
                place(0, dc), h : h + 8
            ].astype(F32)
        top = edge[place(-1, dc)].astype(F32)
        low = edge[place(1, dc)].astype(F32)
        for k in range(3):
            for line, first in ((top[height - 3 + k : height - 2 + k], k), (low[k : k + 1], 3 + height + k)):
                ext[j, first * padded + at : first * padded + at + 1, :] = line

    for k in (0, 1, 2, height + 3, height + 4, height + 5):
        beside(k)
    lane = iota((8, 4 * CH), 1)
    for h in range(0, height, 8):
        for side, at, j in ((0, 0, padded - 1), (1, groups - 1, groups)):
            spot = pl.ds((3 + h) * padded + at, 8, stride=padded)
            chosen = lane >= 3 * CH if side == 0 else lane < CH
            came = edge[place(0, -1 if side == 0 else 1), h : h + 8].astype(F32)
            ext[2, spot, :] = jnp.where(chosen, came, ext[2, spot, :])

    lhs = jnp.concatenate(
        [
            jnp.concatenate([ext[j, line_of(2 * k + e), :] for e in range(4) for j in range(3)], axis=1)
            for k in range(half + 2)
        ],
        axis=0,
    ).astype(BF16)
    conv = jnp.dot(lhs, tdeb[...], preferred_element_type=F32)

    def column(line, left, right):
        spot = iota((padded, groups), 0)
        own = jnp.sum(
            jnp.where(spot == iota((padded, groups), 1), jnp.broadcast_to(line, (padded, groups)), 0.0),
            axis=1, keepdims=True,
        )
        spot = iota((padded, 1), 0)
        own = jnp.where(spot == padded - 1, jnp.broadcast_to(left[:, groups - 1 :], (padded, 1)), own)
        return jnp.where(spot == groups, jnp.broadcast_to(right[:, :1], (padded, 1)), own)

    blocks = vb_ref.shape[0]

    def flag_row(dr, k):
        rows = [
            vb_ref[k : k + 1, :] if (dr, dc) == (0, 0) else flags[place(dr, dc), k : k + 1, :]
            for dc in (-1, 0, 1)
        ]
        left, line, right = [row.astype(F32) for row in rows]
        return column(line, left, right)

    masks = [flag_row(-1, blocks - 1)] + [flag_row(0, k) for k in range(blocks)] + [flag_row(1, 0)]
    deblock_bias = jnp.concatenate([db_ref[...]] * 4, axis=1)
    per = half // blocks
    for k in range(half + 2):
        part = conv[k * padded : (k + 1) * padded]
        which = 0 if k == 0 else blocks + 1 if k == half + 1 else 1 + (k - 1) // per
        pooled[k] = (
            part[:, 4 * CH :] + masks[which] * (part[:, : 4 * CH] + deblock_bias)
        ).astype(BF16)

    def band_copy(to):
        return pltpu.make_async_remote_copy(
            src_ref=pooled.at[pl.ds(to * stride, stride + 2)],
            dst_ref=bands_in.at[me],
            send_sem=band_send.at[to],
            recv_sem=band_recv.at[me],
            device_id={"tm": to},
            device_id_type=MESH,
        )

    def band_arrival(source):
        return pltpu.make_async_remote_copy(
            src_ref=pooled.at[pl.ds(0, stride + 2)],
            dst_ref=bands_in.at[source],
            send_sem=band_send.at[source],
            recv_sem=band_recv.at[source],
            device_id={"tm": source},
            device_id_type=MESH,
        )

    order = [jnp.where(me > k, k, k + 1) for k in range(n - 1)]
    for to in order:
        band_copy(to).start()

    @pl.when(me >= n // 2)
    def _():
        encoder_matrix(ew_ref, tenc)

    slots = []
    for t in range(n):
        if n <= 8:
            slot = jnp.int32(0)
            for s in range(n):
                slot = jnp.where(owner_ref[s] == t, s, slot)
        else:
            slot = lax.fori_loop(
                0, n, lambda s, held: jnp.where(owner_ref[s] == t, s, held), jnp.int32(0)
            )
        slots.append(slot)

    def encode(frames, lines_in):
        rows = []
        for lines_of_frame in lines_in:
            shifted = []
            for own in lines_of_frame:
                side = jnp.where(
                    lanes_of >= 3 * CH,
                    pltpu.roll(own, 1, 0),
                    jnp.where(lanes_of < CH, pltpu.roll(own, padded - 1, 0), 0.0),
                )
                shifted.append(jnp.concatenate([own, side], axis=1))
            rows += [jnp.concatenate(shifted[k : k + 3], axis=1) for k in range(stride)]
        found = jnp.dot(
            jnp.concatenate(rows, axis=0).astype(BF16), tenc[...], preferred_element_type=F32
        ).reshape(len(frames), stride, padded, 12 * OUTC)
        for k, frame in enumerate(frames):
            product[frame] = found[k]

    encode([me], [[pooled[me * stride + k].astype(F32) for k in range(stride + 2)]])
    for source in order:
        band_arrival(source).wait_recv()
    encode(order, [[bands_in[s, k].astype(F32) for k in range(stride + 2)] for s in order])

    width = 4 * OUTC
    encoder_bias = jnp.concatenate([eb_ref[...]] * 4, axis=1)
    for t in range(1, n):
        for k in range(stride):
            total = encoder_bias
            for lag in range(3):
                total = total + product[slots[max(t - lag, 0)], k, :, lag * width : (lag + 1) * width]
            for j in range(2):
                lines[j, line_of((t - 1) * stride + k), :] = total[:, j * 4 * CH : (j + 1) * 4 * CH]
    for h in range(0, (n - 1) * stride, 8):
        count = min(8, (n - 1) * stride - h)
        for q in range(2 * groups):
            out_ref[h : h + count, q * 4 * CH : (q + 1) * 4 * CH] = lines[
                q % 2, pl.ds(h * padded + q // 2, count, stride=padded), :
            ].astype(BF16)

    for dr, dc in DIRECTIONS:

        @pl.when(exists(dr, dc))
        def _():
            for copy in copies(dr, dc):
                copy.wait_send()

    for d in range(1, n):
        band_copy(lax.rem(me + d, n)).wait_send()


def on_device(
    sizes, frames, owner_map, valid_blocks, deblock_weight, deblock_bias, encoder_weight, encoder_bias
):
    n = sizes[0]
    _, height, lanes = frames.shape
    raw = frames[0]
    groups = lanes // (8 * CH)
    padded = -(-(groups + 2) // 8) * 8
    blocks = valid_blocks.shape[1]
    half = height // 2
    stride = half // n
    vmem = pl.BlockSpec(memory_space=pltpu.VMEM)
    operands = (
        owner_map, raw, valid_blocks[0], deblock_weight.T, deblock_bias[None], encoder_weight.T,
        encoder_bias[None],
    )
    encoded = pl.pallas_call(
        functools.partial(kernel, sizes),
        out_shape=jax.ShapeDtypeStruct(((n - 1) * stride, groups * 4 * OUTC), BF16),
        in_specs=[pl.BlockSpec(memory_space=pltpu.HBM)] * 7,
        out_specs=vmem,
        scratch_shapes=[
            pltpu.SMEM((n,), jnp.int32),
            pltpu.VMEM((height, lanes), BF16),
            pltpu.VMEM((blocks, groups), jnp.int32),
            pltpu.VMEM((CH, 9 * CH), BF16),
            pltpu.VMEM((1, CH), F32),
            pltpu.VMEM((OUTC, 27 * CH), BF16),
            pltpu.VMEM((1, OUTC), F32),
            pltpu.VMEM((3, (height + 6) * padded, 4 * CH), F32),
            pltpu.VMEM((2, 3, groups, 8 * CH), BF16),
            pltpu.VMEM((2, 3, groups, 8 * CH), BF16),
            pltpu.VMEM((9, height, 4 * CH), BF16),
            pltpu.VMEM((9, blocks, groups), jnp.int32),
            pltpu.VMEM((48 * CH, 8 * CH), BF16),
            pltpu.VMEM((24 * CH, 12 * OUTC), BF16),
            pltpu.VMEM((half + 2, padded, 4 * CH), BF16),
            pltpu.VMEM((n, stride + 2, padded, 4 * CH), BF16),
            pltpu.VMEM((n, stride, padded, 12 * OUTC), F32),
            pltpu.VMEM((2, (n - 1) * stride * padded, 4 * CH), F32),
            pltpu.SemaphoreType.DMA((7,)),
            pltpu.SemaphoreType.DMA((9, 2)),
            pltpu.SemaphoreType.DMA((9, 2)),
            pltpu.SemaphoreType.DMA((n,)),
            pltpu.SemaphoreType.DMA((n,)),
        ],
        compiler_params=pltpu.CompilerParams(
            collective_id=0, has_side_effects=True, vmem_limit_bytes=40 * 1024 * 1024
        ),
    )(*[pltpu.with_memory_space_constraint(operand, pltpu.HBM) for operand in operands])
    return encoded.reshape(n - 1, 1, stride, groups * 4 * OUTC)


def solution(mesh):
    sizes = (mesh.shape["tm"], mesh.shape["row"], mesh.shape["col"])
    return jax.shard_map(
        functools.partial(on_device, sizes),
        mesh=mesh,
        in_specs=(
            P(("grp", "tm"), "row", "col"),
            P("grp"),
            P(("grp", "tm"), "row", "col"),
            P(),
            P(),
            P(),
            P(),
        ),
        out_specs=P("grp", "row", "tm", "col"),
        check_vma=False,
    )
```

```python
import functools

import jax
import jax.numpy as jnp
from jax import lax
from jax.experimental import pallas as pl
from jax.experimental.pallas import tpu as pltpu
from jax.sharding import PartitionSpec as P

CH = 32
OUTC = 64
MESH = pl.DeviceIdType.MESH
F32 = jnp.float32
BF16 = jnp.bfloat16


def place(dr, dc):
    return (dr + 1) * 3 + dc + 1


DIRECTIONS = [(dr, dc) for dr in (-1, 0, 1) for dc in (-1, 0, 1) if (dr, dc) != (0, 0)]


def iota(shape, dim):
    return lax.broadcasted_iota(jnp.int32, shape, dim)


def spread_taps(taps, spread):
    return lax.dot_general(taps, spread, (((0,), (0,)), ((), ())), preferred_element_type=F32)


def deblock_matrix(dw_ref, t_ref):
    block = iota((CH, 4 * CH), 1) // CH
    same = iota((CH, 4 * CH), 1) - block * CH == iota((CH, 4 * CH), 0)
    spread = same.astype(BF16)
    tiled = spread_taps(dw_ref[...], spread)
    taps = [[tiled[(3 * a + b) * CH : (3 * a + b + 1) * CH] for b in range(3)] for a in range(3)]
    wide = [
        [sum(row[b] for b in (d - 1, d) if 0 <= b < 3) for d in range(4)]
        for row in taps
    ]
    four = [
        [0.25 * sum(wide[a][d] for a in (e - 1, e) if 0 <= a < 3) for d in range(4)]
        for e in range(4)
    ]
    zero = jnp.zeros((CH, 4 * CH), F32)
    quarter = jnp.where(same, 0.25, 0.0)
    means = [jnp.where(block == o, quarter, zero).astype(BF16) for o in range(4)]
    nothing = jnp.zeros((8 * CH, 4 * CH), BF16)
    for e in range(4):
        base = e * 12 * CH

        def put(at, pixel):
            total = zero
            for o in range(4):
                d = pixel - 2 * o + 1
                if 0 <= d < 4:
                    total = jnp.where(block == o, four[e][d], total)
            t_ref[base + at * CH : base + (at + 1) * CH, : 4 * CH] = total.astype(BF16)

        for pixel in range(8):
            put(pixel, pixel)
        put(8, 8)
        put(11, -1)
        t_ref[base + 9 * CH : base + 11 * CH, : 4 * CH] = nothing[: 2 * CH]
        for pixel in range(8):
            t_ref[base + pixel * CH : base + (pixel + 1) * CH, 4 * CH :] = (
                means[pixel // 2] if e in (1, 2) else nothing[:CH]
            )
        t_ref[base + 8 * CH : base + 12 * CH, 4 * CH :] = nothing[: 4 * CH]


def encoder_matrix(ew_ref, t_ref):
    pair = 2 * OUTC
    rows, cols = iota((OUTC, 2 * pair), 0), iota((OUTC, 2 * pair), 1)
    spread = ((cols == rows) | (cols == rows + pair + OUTC)).astype(BF16)
    everything = spread_taps(ew_ref[...], spread).astype(BF16)
    nothing = jnp.zeros((2 * CH, 2 * pair), BF16)
    for lag in range(3):
        for dy in range(3):
            base = dy * 8 * CH
            left = lag * 2 * pair
            first = (lag * 9 + dy * 3) * CH

            def put(at, pixel):
                for side in range(2):
                    total = None
                    for o in (2 * side, 2 * side + 1):
                        d = pixel - o + 1
                        if 0 <= d < 3:
                            tap = everything[
                                first + d * CH : first + (d + 1) * CH, (o % 2) * pair : (o % 2 + 1) * pair
                            ]
                            total = tap if total is None else total + tap
                    if total is None:
                        total = nothing[:CH, :pair]
                    t_ref[
                        base + at * CH : base + (at + 1) * CH, left + side * pair : left + (side + 1) * pair
                    ] = total

            for pixel in range(4):
                put(pixel, pixel)
            put(4, 4)
            put(7, -1)
            t_ref[base + 5 * CH : base + 7 * CH, left : left + 2 * pair] = nothing


def kernel(
    sizes,
    owner_hbm,
    raw_hbm,
    vb_hbm,
    dw_hbm,
    db_hbm,
    ew_hbm,
    eb_hbm,
    out_ref,
    owner_ref,
    raw_ref,
    vb_ref,
    dw_ref,
    db_ref,
    ew_ref,
    eb_ref,
    ext,
    outgoing,
    halo,
    edge,
    flags,
    tdeb,
    tenc,
    pooled,
    bands_in,
    product,
    lines,
    load_sem,
    send_sem,
    recv_sem,
    band_send,
    band_recv,
):
    n, nr, nc = sizes
    height, width = raw_ref.shape
    groups = width // (8 * CH)
    padded = pooled.shape[1]
    half = height // 2
    stride = half // n
    me = lax.axis_index("tm")
    r = lax.axis_index("row")
    c = lax.axis_index("col")

    loads = [
        pltpu.make_async_copy(a, b, load_sem.at[k])
        for k, (a, b) in enumerate(
            (
                (raw_hbm, raw_ref),
                (vb_hbm, vb_ref),
                (dw_hbm, dw_ref),
                (db_hbm, db_ref),
                (ew_hbm, ew_ref),
                (eb_hbm, eb_ref),
                (owner_hbm, owner_ref),
            )
        )
    ]
    for load in loads:
        load.start()

    halo[...] = jnp.zeros_like(halo)
    edge[...] = jnp.zeros_like(edge)
    flags[...] = jnp.zeros_like(flags)

    def exists(dr, dc):
        found = None
        for step, at, count in ((dr, r, nr), (dc, c, nc)):
            if step:
                inside = at > 0 if step < 0 else at < count - 1
                found = inside if found is None else jnp.logical_and(found, inside)
        return found

    def copies(dr, dc):
        here, there = place(dr, dc), place(-dr, -dc)
        to = {}
        if dr:
            to["row"] = r + dr
        if dc:
            to["col"] = c + dc
        if dc:
            lanes = pl.ds(0, 4 * CH) if dc < 0 else pl.ds(raw_ref.shape[1] - 4 * CH, 4 * CH)
            src, dst = raw_ref.at[:, lanes], edge.at[there]
        else:
            src = outgoing.at[0 if dr < 0 else 1]
            dst = halo.at[1 if dr < 0 else 0]
        return [
            pltpu.make_async_remote_copy(
                src_ref=a, dst_ref=b, send_sem=send_sem.at[here, k], recv_sem=recv_sem.at[there, k],
                device_id=to, device_id_type=MESH,
            )
            for k, (a, b) in enumerate(((src, dst), (vb_ref, flags.at[there])))
        ]

    barrier = pltpu.get_barrier_semaphore()
    for dr, dc in DIRECTIONS:
        to = {}
        if dr:
            to["row"] = r + dr
        if dc:
            to["col"] = c + dc

        @pl.when(exists(dr, dc))
        def _():
            pl.semaphore_signal(barrier, inc=1, device_id=to, device_id_type=MESH)

    for d in range(1, n):
        pl.semaphore_signal(
            barrier, inc=1, device_id={"tm": lax.rem(me + d, n)}, device_id_type=MESH
        )
    ext[...] = jnp.zeros_like(ext)

    def line_of(k):
        return pl.ds(k * padded, padded)

    loads[0].wait()
    for h in range(0, height, 8):
        for q in range(2 * groups):
            ext[q % 2, pl.ds((3 + h) * padded + q // 2, 8, stride=padded), :] = raw_ref[
                h : h + 8, q * 4 * CH : (q + 1) * 4 * CH
            ].astype(F32)
    for side, dr in enumerate((-1, 1)):

        @pl.when(exists(dr, 0))
        def _():
            for k in range(3):
                line = line_of(3 + k if dr < 0 else height + k)
                for j in range(2):
                    outgoing[side, k, :, j * 4 * CH : (j + 1) * 4 * CH] = ext[j, line, :][:groups].astype(BF16)

    for load in loads[1:]:
        load.wait()

    @pl.when(me < n // 2)
    def _():
        encoder_matrix(ew_ref, tenc)

    tall = (r > 0).astype(jnp.int32) + (r < nr - 1).astype(jnp.int32) + 1
    broad = (c > 0).astype(jnp.int32) + (c < nc - 1).astype(jnp.int32) + 1
    pl.semaphore_wait(barrier, tall * broad - 1 + n - 1)

    for k in range(2):
        for dr, dc in sorted(DIRECTIONS, key=lambda item: item[1] != 0):

            @pl.when(exists(dr, dc))
            def _():
                copies(dr, dc)[k].start()

    lanes_of = iota((padded, 4 * CH), 1)

    def beside(k):
        before = pltpu.roll(ext[1, line_of(k), :], 1, 0)
        after = pltpu.roll(ext[0, line_of(k), :], padded - 1, 0)
        ext[2, line_of(k), :] = jnp.where(
            lanes_of >= 3 * CH, before, jnp.where(lanes_of < CH, after, 0.0)
        )

    for k in range(3, 3 + height):
        beside(k)
    deblock_matrix(dw_ref, tdeb)

    for dr, dc in DIRECTIONS:

        @pl.when(exists(dr, dc))
        def _():
            for copy in copies(-dr, -dc):
                copy.wait_recv()

    for side, first in ((0, 0), (1, 3 + height)):
        for k in range(3):
            for j in range(2):
                ext[j, pl.ds((first + k) * padded, groups), :] = halo[
                    side, k, :, j * 4 * CH : (j + 1) * 4 * CH
                ].astype(F32)
    for dc, at, j in ((-1, padded - 1, 1), (1, groups, 0)):
        for h in range(0, height, 8):
            ext[j, pl.ds((3 + h) * padded + at, 8, stride=padded), :] = edge[
                place(0, dc), h : h + 8
            ].astype(F32)
        top = edge[place(-1, dc)].astype(F32)
        low = edge[place(1, dc)].astype(F32)
        for k in range(3):
            for line, first in ((top[height - 3 + k : height - 2 + k], k), (low[k : k + 1], 3 + height + k)):
                ext[j, first * padded + at : first * padded + at + 1, :] = line

    for k in (0, 1, 2, height + 3, height + 4, height + 5):
        beside(k)
    lane = iota((8, 4 * CH), 1)
    for h in range(0, height, 8):
        for side, at, j in ((0, 0, padded - 1), (1, groups - 1, groups)):
            spot = pl.ds((3 + h) * padded + at, 8, stride=padded)
            chosen = lane >= 3 * CH if side == 0 else lane < CH
            came = edge[place(0, -1 if side == 0 else 1), h : h + 8].astype(F32)
            ext[2, spot, :] = jnp.where(chosen, came, ext[2, spot, :])

    lhs = jnp.concatenate(
        [
            jnp.concatenate([ext[j, line_of(2 * k + e), :] for e in range(4) for j in range(3)], axis=1)
            for k in range(half + 2)
        ],
        axis=0,
    ).astype(BF16)
    conv = jnp.dot(lhs, tdeb[...], preferred_element_type=F32)

    def column(line, left, right):
        spot = iota((padded, groups), 0)
        own = jnp.sum(
            jnp.where(spot == iota((padded, groups), 1), jnp.broadcast_to(line, (padded, groups)), 0.0),
            axis=1, keepdims=True,
        )
        spot = iota((padded, 1), 0)
        own = jnp.where(spot == padded - 1, jnp.broadcast_to(left[:, groups - 1 :], (padded, 1)), own)
        return jnp.where(spot == groups, jnp.broadcast_to(right[:, :1], (padded, 1)), own)

    blocks = vb_ref.shape[0]

    def flag_row(dr, k):
        rows = [
            vb_ref[k : k + 1, :] if (dr, dc) == (0, 0) else flags[place(dr, dc), k : k + 1, :]
            for dc in (-1, 0, 1)
        ]
        left, line, right = [row.astype(F32) for row in rows]
        return column(line, left, right)

    masks = [flag_row(-1, blocks - 1)] + [flag_row(0, k) for k in range(blocks)] + [flag_row(1, 0)]
    deblock_bias = jnp.concatenate([db_ref[...]] * 4, axis=1)
    per = half // blocks
    for k in range(half + 2):
        part = conv[k * padded : (k + 1) * padded]
        which = 0 if k == 0 else blocks + 1 if k == half + 1 else 1 + (k - 1) // per
        pooled[k] = (
            part[:, 4 * CH :] + masks[which] * (part[:, : 4 * CH] + deblock_bias)
        ).astype(BF16)

    def band_copy(to):
        return pltpu.make_async_remote_copy(
            src_ref=pooled.at[pl.ds(to * stride, stride + 2)],
            dst_ref=bands_in.at[me],
            send_sem=band_send.at[to],
            recv_sem=band_recv.at[me],
            device_id={"tm": to},
            device_id_type=MESH,
        )

    def band_arrival(source):
        return pltpu.make_async_remote_copy(
            src_ref=pooled.at[pl.ds(0, stride + 2)],
            dst_ref=bands_in.at[source],
            send_sem=band_send.at[source],
            recv_sem=band_recv.at[source],
            device_id={"tm": source},
            device_id_type=MESH,
        )

    order = [jnp.where(me > k, k, k + 1) for k in range(n - 1)]
    for to in order:
        band_copy(to).start()

    @pl.when(me >= n // 2)
    def _():
        encoder_matrix(ew_ref, tenc)

    slots = []
    for t in range(n):
        if n <= 8:
            slot = jnp.int32(0)
            for s in range(n):
                slot = jnp.where(owner_ref[s] == t, s, slot)
        else:
            slot = lax.fori_loop(
                0, n, lambda s, held: jnp.where(owner_ref[s] == t, s, held), jnp.int32(0)
            )
        slots.append(slot)

    def encode(frames, lines_in):
        rows = []
        for lines_of_frame in lines_in:
            shifted = []
            for own in lines_of_frame:
                side = jnp.where(
                    lanes_of >= 3 * CH,
                    pltpu.roll(own, 1, 0),
                    jnp.where(lanes_of < CH, pltpu.roll(own, padded - 1, 0), 0.0),
                )
                shifted.append(jnp.concatenate([own, side], axis=1))
            rows += [jnp.concatenate(shifted[k : k + 3], axis=1) for k in range(stride)]
        found = jnp.dot(
            jnp.concatenate(rows, axis=0).astype(BF16), tenc[...], preferred_element_type=F32
        ).reshape(len(frames), stride, padded, 12 * OUTC)
        for k, frame in enumerate(frames):
            product[frame] = found[k]

    encode([me], [[pooled[me * stride + k].astype(F32) for k in range(stride + 2)]])
    for batch in (order[:-1], order[-1:]):
        for source in batch:
            band_arrival(source).wait_recv()
        if batch:
            encode(batch, [[bands_in[s, k].astype(F32) for k in range(stride + 2)] for s in batch])

    width = 4 * OUTC
    encoder_bias = jnp.concatenate([eb_ref[...]] * 4, axis=1)
    for t in range(1, n):
        for k in range(stride):
            total = encoder_bias
            for lag in range(3):
                total = total + product[slots[max(t - lag, 0)], k, :, lag * width : (lag + 1) * width]
            for j in range(2):
                lines[j, line_of((t - 1) * stride + k), :] = total[:, j * 4 * CH : (j + 1) * 4 * CH]
    for h in range(0, (n - 1) * stride, 8):
        count = min(8, (n - 1) * stride - h)
        for q in range(2 * groups):
            out_ref[h : h + count, q * 4 * CH : (q + 1) * 4 * CH] = lines[
                q % 2, pl.ds(h * padded + q // 2, count, stride=padded), :
            ].astype(BF16)

    for dr, dc in DIRECTIONS:

        @pl.when(exists(dr, dc))
        def _():
            for copy in copies(dr, dc):
                copy.wait_send()

    for d in range(1, n):
        band_copy(lax.rem(me + d, n)).wait_send()


def on_device(
    sizes, frames, owner_map, valid_blocks, deblock_weight, deblock_bias, encoder_weight, encoder_bias
):
    n = sizes[0]
    _, height, lanes = frames.shape
    raw = frames[0]
    groups = lanes // (8 * CH)
    padded = -(-(groups + 2) // 8) * 8
    blocks = valid_blocks.shape[1]
    half = height // 2
    stride = half // n
    vmem = pl.BlockSpec(memory_space=pltpu.VMEM)
    operands = (
        owner_map, raw, valid_blocks[0], deblock_weight.T, deblock_bias[None], encoder_weight.T,
        encoder_bias[None],
    )
    encoded = pl.pallas_call(
        functools.partial(kernel, sizes),
        out_shape=jax.ShapeDtypeStruct(((n - 1) * stride, groups * 4 * OUTC), BF16),
        in_specs=[pl.BlockSpec(memory_space=pltpu.HBM)] * 7,
        out_specs=vmem,
        scratch_shapes=[
            pltpu.SMEM((n,), jnp.int32),
            pltpu.VMEM((height, lanes), BF16),
            pltpu.VMEM((blocks, groups), jnp.int32),
            pltpu.VMEM((CH, 9 * CH), BF16),
            pltpu.VMEM((1, CH), F32),
            pltpu.VMEM((OUTC, 27 * CH), BF16),
            pltpu.VMEM((1, OUTC), F32),
            pltpu.VMEM((3, (height + 6) * padded, 4 * CH), F32),
            pltpu.VMEM((2, 3, groups, 8 * CH), BF16),
            pltpu.VMEM((2, 3, groups, 8 * CH), BF16),
            pltpu.VMEM((9, height, 4 * CH), BF16),
            pltpu.VMEM((9, blocks, groups), jnp.int32),
            pltpu.VMEM((48 * CH, 8 * CH), BF16),
            pltpu.VMEM((24 * CH, 12 * OUTC), BF16),
            pltpu.VMEM((half + 2, padded, 4 * CH), BF16),
            pltpu.VMEM((n, stride + 2, padded, 4 * CH), BF16),
            pltpu.VMEM((n, stride, padded, 12 * OUTC), F32),
            pltpu.VMEM((2, (n - 1) * stride * padded, 4 * CH), F32),
            pltpu.SemaphoreType.DMA((7,)),
            pltpu.SemaphoreType.DMA((9, 2)),
            pltpu.SemaphoreType.DMA((9, 2)),
            pltpu.SemaphoreType.DMA((n,)),
            pltpu.SemaphoreType.DMA((n,)),
        ],
        compiler_params=pltpu.CompilerParams(
            collective_id=0, has_side_effects=True, vmem_limit_bytes=40 * 1024 * 1024
        ),
    )(*[pltpu.with_memory_space_constraint(operand, pltpu.HBM) for operand in operands])
    return encoded.reshape(n - 1, 1, stride, groups * 4 * OUTC)


def solution(mesh):
    sizes = (mesh.shape["tm"], mesh.shape["row"], mesh.shape["col"])
    return jax.shard_map(
        functools.partial(on_device, sizes),
        mesh=mesh,
        in_specs=(
            P(("grp", "tm"), "row", "col"),
            P("grp"),
            P(("grp", "tm"), "row", "col"),
            P(),
            P(),
            P(),
            P(),
        ),
        out_specs=P("grp", "row", "tm", "col"),
        check_vma=False,
    )
```
